256 devices in a mesh: tm: 8 (over y, core), seq: 32 (over x, z).
Axes of the slice: x: 4, y: 4, z: 8, core: 2. Of those that a mesh axis runs over, the one named last changes fastest.
Arguments:
- queries: bfloat16 [65536, 4096], P(('tm', 'seq')), may hold values from -9 to 9
- keys_values: bfloat16 [2, 65536, 4096], P(None, ('tm', 'seq')), may hold values from -6 to 6
- extents: int32 [3, 32], replicated, may hold values from 0 to 2
- tile_lists: int32 [512, 16], P('tm'), may hold values from 0 to 511, as said below
Outputs:
- attended: bfloat16 [65536, 4096], P(('tm', 'seq'))
The draws below stay inside these ranges and needn't reach their ends.
Inputs may be any that keep to these rules, and one draw needn't show every extreme that they name: `tile_lists`: slot 0 of row g is g itself; the other 15 entries of a row are different tiles of g's window, 3 tiles along each of time, height and width, centred on g and moved inward at the grid's edges.
All inputs are finite; a program needn't handle non-finite values.
Results may differ from the reference program's by a relative error of at most 0.0065.
Values may be sent and summed in bfloat16 or wider, within the bound.
No kernel may reach another device: no remote copies, remote signals or barrier semaphores. Data moves between devices by JAX's collectives and lax.ppermute only.
A program may use at most 128 MiB of HBM per device.

```python
import jax
import jax.numpy as jnp
from jax import lax

HEAD_DIM = 128
TILE = 128
GH = 4
GW = 8
KSEL = 16
HEADS = 32
TOKENS = 65536
GT = 16
TILES = 512


def draw_queries(key, part):
    key = jax.random.fold_in(key, 11)
    full_shape = (TOKENS, HEADS * HEAD_DIM)
    return jnp.clip(jax.random.normal(key, full_shape, jnp.float32), -6.0, 6.0).astype(jnp.bfloat16)


def draw_keys_values(key, part):
    key = jax.random.fold_in(key, 23)
    key_part, value_part = jax.random.split(key)
    full_shape = (TOKENS, HEADS * HEAD_DIM)
    key_rows = jnp.clip(jax.random.normal(key_part, full_shape, jnp.float32), -6.0, 6.0)
    value_rows = jnp.clip(jax.random.normal(value_part, full_shape, jnp.float32), -6.0, 6.0)
    return jnp.stack([key_rows, value_rows]).astype(jnp.bfloat16)


def draw_tile_lists(key, part):
    key = jax.random.fold_in(key, 37)
    tile_ids = jnp.arange(TILES, dtype=jnp.int32)
    frame_tiles = GH * GW
    tile_time = tile_ids // frame_tiles
    tile_row = tile_ids // GW % GH
    tile_column = tile_ids % GW
    start_time = jnp.clip(tile_time - 1, 0, GT - 3)
    start_row = jnp.clip(tile_row - 1, 0, GH - 3)
    start_column = jnp.clip(tile_column - 1, 0, GW - 3)
    offsets = jnp.arange(27, dtype=jnp.int32)
    candidates = (start_time[:, None] + offsets // 9) * frame_tiles + (start_row[:, None] + offsets // 3 % 3) * GW + start_column[:, None] + offsets % 3
    tile_keys = jax.random.split(key, TILES)

    def shuffle_one(one_key):
        return jax.random.permutation(one_key, 27)
    shuffles = jax.vmap(shuffle_one)(tile_keys)
    shuffled = jnp.take_along_axis(candidates, shuffles, axis=1)
    is_self = (shuffled == tile_ids[:, None]).astype(jnp.int32)
    slot_order = jnp.argsort(is_self, axis=1, stable=True)
    others = jnp.take_along_axis(shuffled, slot_order, axis=1)[:, :KSEL - 1]
    return jnp.concatenate([tile_ids[:, None], others], axis=1).astype(jnp.int32)


def set_ends(result, own_key, smallest, top_value):
    shape = result.shape
    spot = [jax.random.randint(jax.random.fold_in(own_key, axis), (), 0, shape[axis]) for axis in range(len(shape))]
    result = result.at[tuple(spot)].set(smallest)
    longest = shape.index(max(shape))
    spot[longest] = (spot[longest] + 1) % shape[longest]
    return result.at[tuple(spot)].set(top_value)


def setup_inputs(seed: int = 0) -> dict:
    key_of = jax.random.split(jax.random.key(seed), 5)
    return {
        "queries": draw_queries(jax.random.fold_in(key_of[4], 71), 0),
        "keys_values": draw_keys_values(jax.random.fold_in(key_of[4], 71), 0),
        "extents": set_ends(jax.random.randint(key_of[2], (3, HEADS), 0, 3), jax.random.fold_in(key_of[2], 1), 0, 2).astype(jnp.int32),
        "tile_lists": draw_tile_lists(jax.random.fold_in(key_of[4], 71), 0),
    }


def tile_place(tile_ids):
    return tile_ids // (GH * GW), (tile_ids // GW) % GH, tile_ids % GW


def divisor_below(amount, limit_size):
    best_size = 1
    for candidate in range(1, min(amount, limit_size) + 1):
        if amount % candidate == 0:
            best_size = candidate
    return best_size


def attend_block(inputs, key_tiles, value_tiles):
    queries_block, lists_block, live_block = inputs
    gathered_keys = jnp.take(key_tiles, lists_block, axis=0).astype(jnp.float32)
    gathered_values = jnp.take(value_tiles, lists_block, axis=0).astype(jnp.float32)
    scores = jnp.einsum("bid,bkjd->bikj", queries_block.astype(jnp.float32), gathered_keys) * (HEAD_DIM ** -0.5)
    alive_grid = live_block[:, None, :, None]
    block_top = jnp.max(jnp.where(alive_grid, scores, -jnp.inf), axis=(2, 3), keepdims=True)
    weights = jnp.where(alive_grid, jnp.exp(scores - block_top), 0.0)
    totals = jnp.sum(weights, axis=(2, 3))
    rounded = lax.optimization_barrier(weights.astype(jnp.bfloat16))
    mixed = jnp.einsum("bikj,bkjd->bid", rounded.astype(jnp.float32), gathered_values)
    return (mixed / totals[..., None]).astype(jnp.bfloat16)


def reference(queries, keys_values, extents, tile_lists):
    tile_total = tile_lists.shape[0]
    shaped_queries = queries.reshape(tile_total, TILE, HEADS, HEAD_DIM)
    shaped_keys = keys_values[0].reshape(tile_total, TILE, HEADS, HEAD_DIM)
    shaped_values = keys_values[1].reshape(tile_total, TILE, HEADS, HEAD_DIM)
    query_ids = jnp.arange(tile_total, dtype=jnp.int32)
    query_time, query_row, query_column = tile_place(query_ids)
    listed_time, listed_row, listed_column = tile_place(tile_lists)
    group_size = divisor_below(tile_total, 64)
    groups = tile_total // group_size

    def one_head(head_index):
        reaches = lax.dynamic_index_in_dim(extents, head_index, 1, keepdims=False)
        live_slots = (jnp.abs(listed_time - query_time[:, None]) <= reaches[0]) & (jnp.abs(listed_row - query_row[:, None]) <= reaches[1]) & (jnp.abs(listed_column - query_column[:, None]) <= reaches[2])
        query_tiles = lax.dynamic_index_in_dim(shaped_queries, head_index, 2, keepdims=False)
        key_tiles = lax.dynamic_index_in_dim(shaped_keys, head_index, 2, keepdims=False)
        value_tiles = lax.dynamic_index_in_dim(shaped_values, head_index, 2, keepdims=False)

        def one_group(inputs):
            return attend_block(inputs, key_tiles, value_tiles)

        outputs = lax.map(one_group, (query_tiles.reshape(groups, group_size, TILE, HEAD_DIM), tile_lists.reshape(groups, group_size, KSEL), live_slots.reshape(groups, group_size, KSEL)))
        return outputs.reshape(tile_total, TILE, HEAD_DIM)

    heads_out = lax.map(one_head, jnp.arange(HEADS, dtype=jnp.int32))
    return heads_out.transpose(1, 2, 0, 3).reshape(TOKENS, HEADS * HEAD_DIM)
```

```python
import functools

import jax
import jax.numpy as jnp
from jax import lax
from jax.experimental import pallas as pl
from jax.experimental.pallas import tpu as pltpu
from jax.sharding import PartitionSpec as P

HEAD_DIM = 128
TILE = 128
GH = 4
GW = 8
FRAME = GH * GW
KSEL = 16
CHUNKS = 2
EXP2_SCALE = HEAD_DIM ** (-0.5) * 1.4426950408889634
DEAD = -1e30


def attend_kernel(chunk, slots_ref, query_ref, left_ref, own_ref, right_ref, out_ref, held, sems):
    step = pl.program_id(0)
    pairs = own_ref.shape[0]
    rim = left_ref.shape[0]

    @pl.when(step == 0)
    def _():
        copies = [
            pltpu.make_async_copy(own_ref, held.at[pl.ds(rim, pairs)], sems.at[0]),
            pltpu.make_async_copy(left_ref, held.at[pl.ds(0, rim)], sems.at[1]),
            pltpu.make_async_copy(right_ref, held.at[pl.ds(rim + pairs, rim)], sems.at[2]),
        ]
        for copy in copies:
            copy.start()
        for copy in copies:
            copy.wait()

    tiles_step = query_ref.shape[0]
    ones = jnp.ones((2 * TILE, HEAD_DIM), jnp.bfloat16)
    for tile in range(tiles_step):
        row = (step * tiles_step + tile) * CHUNKS + chunk
        query = query_ref[tile]
        scores = []
        places = []
        top = None
        for slot in range(0, KSEL, 2):
            codes = [slots_ref[row, slot + i] for i in range(2)]
            tiles = [code & 127 for code in codes]
            bias = [jnp.where(code >= 128, DEAD, 0.0) for code in codes]
            places.append((tiles, bias))
            keys = jnp.concatenate([held[k >> 1, 0, k & 1] for k in tiles], axis=0)
            score = lax.dot_general(
                query, keys, (((1,), (1,)), ((), ())), preferred_element_type=jnp.float32
            )
            score = [score[:, i * TILE : (i + 1) * TILE] + bias[i] for i in range(2)]
            scores.append(score)
            best = jnp.maximum(score[0], score[1])
            top = best if top is None else jnp.maximum(top, best)
        top = jnp.max(top, axis=1, keepdims=True)
        mixed = None
        for score, (tiles, bias) in zip(scores, places):
            weights = jnp.concatenate(
                [jnp.exp2((part - top) * EXP2_SCALE).astype(jnp.bfloat16) for part in score], axis=1
            )
            values = jnp.concatenate([held[k >> 1, 1, k & 1] for k in tiles], axis=0)
            part = jnp.dot(
                weights,
                jnp.concatenate([values, ones], axis=1),
                preferred_element_type=jnp.float32,
            )
            mixed = part if mixed is None else mixed + part
        out_ref[tile] = (mixed[:, :HEAD_DIM] / mixed[:, HEAD_DIM:]).astype(jnp.bfloat16)


def attend(chunk, slots, query_tiles, left, own, right):
    count = query_tiles.shape[0]
    tiles_step = 2
    pairs = own.shape[0]
    whole = pl.BlockSpec(memory_space=pl.ANY)
    return pl.pallas_call(
        functools.partial(attend_kernel, chunk),
        grid=(count // tiles_step,),
        in_specs=[
            pl.BlockSpec(memory_space=pltpu.SMEM),
            pl.BlockSpec((tiles_step, TILE, HEAD_DIM), lambda i: (i, 0, 0)),
            whole,
            whole,
            whole,
        ],
        out_specs=pl.BlockSpec((tiles_step, TILE, HEAD_DIM), lambda i: (i, 0, 0)),
        out_shape=jax.ShapeDtypeStruct((count, TILE, HEAD_DIM), jnp.bfloat16),
        scratch_shapes=[
            pltpu.VMEM((pairs + 2 * left.shape[0],) + own.shape[1:], jnp.bfloat16),
            pltpu.SemaphoreType.DMA((3,)),
        ],
        compiler_params=pltpu.CompilerParams(vmem_limit_bytes=40 * 1024 * 1024),
        cost_estimate=pl.CostEstimate(
            flops=count * KSEL * TILE * TILE * HEAD_DIM * 4,
            bytes_accessed=12 * 1024 * 1024,
            transcendentals=count * KSEL * TILE * TILE,
        ),
    )(slots, query_tiles, left, own, right)


def tile_place(tile_ids):
    return (tile_ids // FRAME, tile_ids // GW % GH, tile_ids % GW)


def slot_codes(extents, tile_lists, head, first_tile):
    reaches = lax.dynamic_slice_in_dim(extents, head, 1, axis=1)[:, 0]
    query_ids = first_tile + jnp.arange(tile_lists.shape[0], dtype=jnp.int32)
    query_time, query_row, query_column = tile_place(query_ids)
    listed_time, listed_row, listed_column = tile_place(tile_lists)
    live = (
        (jnp.abs(listed_time - query_time[:, None]) <= reaches[0])
        & (jnp.abs(listed_row - query_row[:, None]) <= reaches[1])
        & (jnp.abs(listed_column - query_column[:, None]) <= reaches[2])
    )
    local = tile_lists - (first_tile - FRAME)
    return jnp.where(live, local, local + 128)


def exchange(blocks):
    return lax.all_to_all(blocks, "seq", split_axis=0, concat_axis=0, tiled=True)


def per_device(queries, keys_values, extents, tile_lists):
    seq_size = lax.axis_size("seq")
    tm_size = lax.axis_size("tm")
    tok_dev, width_all = queries.shape
    heads = width_all // HEAD_DIM
    slab_tiles = tok_dev * seq_size // TILE
    first_tile = lax.axis_index("tm") * slab_tiles
    head = lax.axis_index("seq")

    pairs_by_head = keys_values.reshape(2, tok_dev, heads, HEAD_DIM).transpose(2, 0, 1, 3)
    own = exchange(pairs_by_head).reshape(seq_size, 2, CHUNKS, TILE, HEAD_DIM)
    half = seq_size // 2
    ends = tm_size - 1
    left = lax.ppermute(own[half:], "tm", [(i, i + 1) for i in range(ends)])
    right = lax.ppermute(own[:half], "tm", [(i + 1, i) for i in range(ends)])

    queries_by_head = queries.reshape(CHUNKS, TILE, heads, HEAD_DIM).transpose(0, 2, 1, 3)
    slots = slot_codes(extents, tile_lists, head, first_tile)
    outputs = []
    for chunk in range(CHUNKS):
        query_tiles = exchange(queries_by_head[chunk])
        attended = attend(chunk, slots, query_tiles, left, own, right)
        outputs.append(exchange(attended))
    stacked = jnp.stack(outputs)
    return stacked.transpose(0, 2, 1, 3).reshape(tok_dev, width_all)


def solution(mesh):
    placed = (P(("tm", "seq"), None), P(None, ("tm", "seq"), None), P(), P("tm", None))
    return jax.shard_map(
        per_device, mesh=mesh, in_specs=placed, out_specs=P(("tm", "seq"), None), check_vma=False
    )
```

```python
import functools

import jax
import jax.numpy as jnp
from jax import lax
from jax.experimental import pallas as pl
from jax.experimental.pallas import tpu as pltpu
from jax.sharding import PartitionSpec as P

HEAD_DIM = 128
TILE = 128
FRAME = 32
KSEL = 16
CHUNKS = 2
HEADS_STEP = 4
NO_TILE = 128
EXP2_SCALE = HEAD_DIM ** (-0.5) * 1.4426950408889634
MIB = 1024 * 1024


def split_kernel(extents, list_ref, query_ref, pair_ref, block_ref, second_ref, id_ref):
    for head in range(block_ref.shape[0]):
        columns = slice(head * HEAD_DIM, (head + 1) * HEAD_DIM)
        for part in range(2):
            for half in range(CHUNKS):
                rows = slice(half * TILE, (half + 1) * TILE)
                block_ref[head, part * CHUNKS + half] = pair_ref[part, rows, columns]
        block_ref[head, 2 * CHUNKS] = query_ref[0:TILE, columns]
        second_ref[head] = query_ref[TILE : 2 * TILE, columns]

    @pl.when(pl.program_id(0) == 0)
    def _():
        head = lax.axis_index("seq")
        listed = list_ref[...]
        first = lax.axis_index("tm") * listed.shape[1]
        tiles = first + lax.broadcasted_iota(jnp.int32, listed.shape, 1)
        live = None
        for axis, (low, mask) in enumerate(((5, 15), (3, 3), (0, 7))):
            gap = jnp.abs(((listed >> low) & mask) - ((tiles >> low) & mask))
            near = gap <= extents[axis, head]
            live = near if live is None else live & near
        shift = first - FRAME
        id_ref[0] = jnp.where(live, listed, tiles) - shift
        id_ref[1] = jnp.where(live, listed - shift, NO_TILE)


def split_heads(queries, keys_values, extents, tile_lists):
    tok_dev, width_all = queries.shape
    heads = width_all // HEAD_DIM
    width = HEADS_STEP * HEAD_DIM
    parts = 2 * CHUNKS + 1
    slots, rows = tile_lists.shape[1], tile_lists.shape[0]
    return pl.pallas_call(
        split_kernel,
        grid=(heads // HEADS_STEP,),
        in_specs=[
            pl.BlockSpec(memory_space=pltpu.SMEM),
            pl.BlockSpec((slots, rows), lambda i: (0, 0)),
            pl.BlockSpec((tok_dev, width), lambda i: (0, i)),
            pl.BlockSpec((2, tok_dev, width), lambda i: (0, 0, i)),
        ],
        out_specs=[
            pl.BlockSpec((HEADS_STEP, parts, TILE, HEAD_DIM), lambda i: (i, 0, 0, 0)),
            pl.BlockSpec((HEADS_STEP, TILE, HEAD_DIM), lambda i: (i, 0, 0)),
            pl.BlockSpec((2, slots, rows), lambda i: (0, 0, 0)),
        ],
        out_shape=[
            jax.ShapeDtypeStruct((heads, parts, TILE, HEAD_DIM), jnp.bfloat16),
            jax.ShapeDtypeStruct((heads, TILE, HEAD_DIM), jnp.bfloat16),
            jax.ShapeDtypeStruct((2, slots, rows), jnp.int32),
        ],
        compiler_params=pltpu.CompilerParams(vmem_limit_bytes=60 * MIB),
    )(extents, tile_lists.T, queries, keys_values)


def join_kernel(first_ref, second_ref, out_ref):
    for head in range(first_ref.shape[0]):
        columns = slice(head * HEAD_DIM, (head + 1) * HEAD_DIM)
        out_ref[0:TILE, columns] = first_ref[head]
        out_ref[TILE : 2 * TILE, columns] = second_ref[head]


def join_heads(first, second):
    heads = first.shape[0]
    width = HEADS_STEP * HEAD_DIM
    block = pl.BlockSpec((HEADS_STEP, TILE, HEAD_DIM), lambda i: (i, 0, 0))
    return pl.pallas_call(
        join_kernel,
        grid=(heads // HEADS_STEP,),
        in_specs=[block, block],
        out_specs=pl.BlockSpec((2 * TILE, width), lambda i: (0, i)),
        out_shape=jax.ShapeDtypeStruct((2 * TILE, heads * HEAD_DIM), jnp.bfloat16),
        compiler_params=pltpu.CompilerParams(vmem_limit_bytes=60 * MIB),
    )(first, second)


def attend_kernel(
    chunk,
    query_part,
    slot_ids,
    query_hbm,
    left_hbm,
    own_hbm,
    right_hbm,
    out_ref,
    keys,
    values,
    query,
    marks,
    scores,
    tops,
    sems,
):
    pairs = own_hbm.shape[0]
    rim = left_hbm.shape[0]
    places = ((own_hbm, rim), (left_hbm, 0), (right_hbm, rim + pairs))
    copies = [pltpu.make_async_copy(query_hbm.at[:, query_part], query, sems.at[0])]
    for part, held in enumerate((keys, values)):
        for source, start in places:
            copies.append(
                pltpu.make_async_copy(
                    source.at[:, pl.ds(part * CHUNKS, CHUNKS)],
                    held.at[pl.ds(start, source.shape[0])],
                    sems.at[len(copies)],
                )
            )
    for copy in copies:
        copy.start()
    marks[0] = jnp.ones((TILE, HEAD_DIM), jnp.bfloat16)
    marks[1] = jnp.zeros((TILE, HEAD_DIM), jnp.bfloat16)
    values[NO_TILE // CHUNKS] = jnp.zeros((CHUNKS, TILE, HEAD_DIM), jnp.bfloat16)
    for copy in copies[:4]:
        copy.wait()
    count = query.shape[0]

    def score_pair(row, tile_query, slot):
        ids = [slot_ids[0, slot + i, row] for i in range(2)]
        both = jnp.concatenate([keys[k >> 1, k & 1] for k in ids], axis=0)
        return lax.dot_general(
            tile_query, both, (((1,), (1,)), ((), ())), preferred_element_type=jnp.float32
        )

    def value_pair(row, slot):
        ids = [slot_ids[1, slot + i, row] for i in range(2)]
        return jnp.concatenate(
            [jnp.concatenate([values[k >> 1, k & 1], marks[k >> 7]], axis=1) for k in ids], axis=0
        )

    def fold(best, score):
        score = jnp.maximum(score[:, :TILE], score[:, TILE:])
        return score if best is None else jnp.maximum(best, score)

    def put_top(place, best):
        tops[place] = jnp.broadcast_to(jnp.max(best, axis=1, keepdims=True), (TILE, TILE))

    best = None
    for slot in range(0, KSEL, 2):
        score = score_pair(chunk, query[0], slot)
        scores[0, slot // 2] = score
        best = fold(best, score)
    put_top(0, best)
    for copy in copies[4:]:
        copy.wait()

    def step(turn, carry):
        for now in range(2):
            tile = turn * 2 + now
            later = jnp.minimum(tile + 1, count - 1)
            row, later_row = tile * CHUNKS + chunk, later * CHUNKS + chunk
            top = tops[now]
            top = jnp.concatenate([top, top], axis=1)
            later_query = query[later]
            best = None
            mixed = None
            for slot in range(0, KSEL, 2):
                score = score_pair(later_row, later_query, slot)
                scores[1 - now, slot // 2] = score
                best = fold(best, score)
                weights = jnp.exp2((scores[now, slot // 2] - top) * EXP2_SCALE)
                part = jnp.dot(
                    weights.astype(jnp.bfloat16),
                    value_pair(row, slot),
                    preferred_element_type=jnp.float32,
                )
                mixed = part if mixed is None else mixed + part
            put_top(1 - now, best)
            out_ref[tile] = (mixed[:, :HEAD_DIM] / mixed[:, HEAD_DIM:]).astype(jnp.bfloat16)
        return carry

    lax.fori_loop(0, count // 2, step, 0)


def attend(chunk, ids, query_tiles, query_part, left, own, right):
    count = query_tiles.shape[0]
    held = own.shape[0] + 2 * left.shape[0]
    whole = pl.BlockSpec(memory_space=pl.ANY)
    scalar = pl.BlockSpec(memory_space=pltpu.SMEM)
    return pl.pallas_call(
        functools.partial(attend_kernel, chunk, query_part),
        in_specs=[scalar, whole, whole, whole, whole],
        out_specs=pl.BlockSpec(memory_space=pltpu.VMEM),
        out_shape=jax.ShapeDtypeStruct((count, TILE, HEAD_DIM), jnp.bfloat16),
        scratch_shapes=[
            pltpu.VMEM((held, CHUNKS, TILE, HEAD_DIM), jnp.bfloat16),
            pltpu.VMEM((held + 1, CHUNKS, TILE, HEAD_DIM), jnp.bfloat16),
            pltpu.VMEM((count, TILE, HEAD_DIM), jnp.bfloat16),
            pltpu.VMEM((2, TILE, HEAD_DIM), jnp.bfloat16),
            pltpu.VMEM((2, KSEL // 2, TILE, 2 * TILE), jnp.float32),
            pltpu.VMEM((2, TILE, TILE), jnp.float32),
            pltpu.SemaphoreType.DMA((7,)),
        ],
        compiler_params=pltpu.CompilerParams(vmem_limit_bytes=60 * MIB),
        cost_estimate=pl.CostEstimate(
            flops=count * KSEL * TILE * TILE * HEAD_DIM * 4,
            bytes_accessed=12 * MIB,
            transcendentals=count * KSEL * TILE * TILE,
        ),
    )(ids, query_tiles, left, own, right)


def exchange(blocks):
    return lax.all_to_all(blocks, "seq", split_axis=0, concat_axis=0, tiled=True)


def per_device(queries, keys_values, extents, tile_lists):
    seq_size = lax.axis_size("seq")
    tm_size = lax.axis_size("tm")
    blocks, second, ids = split_heads(queries, keys_values, extents, tile_lists)
    own = exchange(blocks)
    half = seq_size // 2
    ends = tm_size - 1
    rims = 2 * CHUNKS
    left = lax.ppermute(own[half:, :rims], "tm", [(i, i + 1) for i in range(ends)])
    right = lax.ppermute(own[:half, :rims], "tm", [(i + 1, i) for i in range(ends)])

    second = exchange(second)[:, None]
    first_out = exchange(attend(0, ids, own, rims, left, own, right))
    second_out = exchange(attend(1, ids, second, 0, left, own, right))
    return join_heads(first_out, second_out)


def solution(mesh):
    placed = (P(("tm", "seq"), None), P(None, ("tm", "seq"), None), P(), P("tm", None))
    return jax.shard_map(
        per_device, mesh=mesh, in_specs=placed, out_specs=P(("tm", "seq"), None), check_vma=False
    )
```

```python
import functools

import jax
import jax.numpy as jnp
from jax import lax
from jax.experimental import pallas as pl
from jax.experimental.pallas import tpu as pltpu
from jax.sharding import PartitionSpec as P

HEAD_DIM = 128
TILE = 128
FRAME = 32
KSEL = 16
CHUNKS = 2
HEADS_STEP = 16
NO_TILE = 128
EXP2_SCALE = HEAD_DIM ** (-0.5) * 1.4426950408889634
MIB = 1024 * 1024


def split_queries_kernel(query_ref, *block_refs):
    for chunk, block_ref in enumerate(block_refs):
        for head in range(block_ref.shape[0]):
            columns = slice(head * HEAD_DIM, (head + 1) * HEAD_DIM)
            block_ref[head] = query_ref[chunk * TILE : (chunk + 1) * TILE, columns]


def split_queries(queries):
    tok_dev, width_all = queries.shape
    heads = width_all // HEAD_DIM
    return pl.pallas_call(
        split_queries_kernel,
        grid=(heads // HEADS_STEP,),
        in_specs=[pl.BlockSpec((tok_dev, HEADS_STEP * HEAD_DIM), lambda i: (0, i))],
        out_specs=[pl.BlockSpec((HEADS_STEP, TILE, HEAD_DIM), lambda i: (i, 0, 0))] * CHUNKS,
        out_shape=[jax.ShapeDtypeStruct((heads, TILE, HEAD_DIM), jnp.bfloat16)] * CHUNKS,
        compiler_params=pltpu.CompilerParams(vmem_limit_bytes=60 * MIB),
        cost_estimate=pl.CostEstimate(flops=0, bytes_accessed=4 * MIB, transcendentals=0),
    )(queries)


def split_pairs_kernel(extents, list_ref, pair_ref, block_ref, id_ref):
    for head in range(block_ref.shape[0]):
        columns = slice(head * HEAD_DIM, (head + 1) * HEAD_DIM)
        for part in range(2):
            for half in range(CHUNKS):
                rows = slice(half * TILE, (half + 1) * TILE)
                block_ref[head, part * CHUNKS + half] = pair_ref[part, rows, columns]

    @pl.when(pl.program_id(0) == 0)
    def _():
        head = lax.axis_index("seq")
        listed = list_ref[...]
        first = lax.axis_index("tm") * listed.shape[1]
        tiles = first + lax.broadcasted_iota(jnp.int32, listed.shape, 1)
        live = None
        for axis, (low, mask) in enumerate(((5, 15), (3, 3), (0, 7))):
            gap = jnp.abs(((listed >> low) & mask) - ((tiles >> low) & mask))
            near = gap <= extents[axis, head]
            live = near if live is None else live & near
        shift = first - FRAME
        id_ref[0] = jnp.where(live, listed, tiles) - shift
        id_ref[1] = jnp.where(live, listed - shift, NO_TILE)


def split_pairs(keys_values, extents, tile_lists):
    _, tok_dev, width_all = keys_values.shape
    heads = width_all // HEAD_DIM
    parts = 2 * CHUNKS
    rows, slots = tile_lists.shape
    return pl.pallas_call(
        split_pairs_kernel,
        grid=(heads // HEADS_STEP,),
        in_specs=[
            pl.BlockSpec(memory_space=pltpu.SMEM),
            pl.BlockSpec((slots, rows), lambda i: (0, 0)),
            pl.BlockSpec((2, tok_dev, HEADS_STEP * HEAD_DIM), lambda i: (0, 0, i)),
        ],
        out_specs=[
            pl.BlockSpec((HEADS_STEP, parts, TILE, HEAD_DIM), lambda i: (i, 0, 0, 0)),
            pl.BlockSpec((2, slots, rows), lambda i: (0, 0, 0)),
        ],
        out_shape=[
            jax.ShapeDtypeStruct((heads, parts, TILE, HEAD_DIM), jnp.bfloat16),
            jax.ShapeDtypeStruct((2, slots, rows), jnp.int32),
        ],
        compiler_params=pltpu.CompilerParams(vmem_limit_bytes=60 * MIB),
    )(extents, tile_lists.T, keys_values)


def join_kernel(first_hbm, second_hbm, out_hbm, held, in_sems, out_sems):
    sources = (first_hbm, second_hbm)
    reads = [
        [
            pltpu.make_async_copy(
                source.at[head],
                held.at[pl.ds(chunk * TILE, TILE), pl.ds(head * HEAD_DIM, HEAD_DIM)],
                in_sems.at[chunk, head],
            )
            for head in range(source.shape[0])
        ]
        for chunk, source in enumerate(sources)
    ]
    for copies in reads:
        for copy in copies:
            copy.start()
    writes = []
    for chunk, copies in enumerate(reads):
        for copy in copies:
            copy.wait()
        rows = pl.ds(chunk * TILE, TILE)
        writes.append(pltpu.make_async_copy(held.at[rows], out_hbm.at[rows], out_sems.at[chunk]))
        writes[-1].start()
    for copy in writes:
        copy.wait()


def join_heads(first, second):
    heads = first.shape[0]
    whole = pl.BlockSpec(memory_space=pl.ANY)
    shape = (CHUNKS * TILE, heads * HEAD_DIM)
    return pl.pallas_call(
        join_kernel,
        in_specs=[whole, whole],
        out_specs=whole,
        out_shape=jax.ShapeDtypeStruct(shape, jnp.bfloat16),
        scratch_shapes=[
            pltpu.VMEM(shape, jnp.bfloat16),
            pltpu.SemaphoreType.DMA((CHUNKS, heads)),
            pltpu.SemaphoreType.DMA((CHUNKS,)),
        ],
        compiler_params=pltpu.CompilerParams(vmem_limit_bytes=60 * MIB),
    )(first, second)


def attend_kernel(
    chunk,
    slot_ids,
    query_hbm,
    left_hbm,
    own_hbm,
    right_hbm,
    out_ref,
    keys,
    values,
    query,
    marks,
    scores,
    tops,
    sems,
):
    pairs = own_hbm.shape[0]
    rim = left_hbm.shape[0]
    places = ((own_hbm, rim), (left_hbm, 0), (right_hbm, rim + pairs))
    copies = [pltpu.make_async_copy(query_hbm, query, sems.at[0])]
    for part, held in enumerate((keys, values)):
        for source, start in places:
            copies.append(
                pltpu.make_async_copy(
                    source.at[:, pl.ds(part * CHUNKS, CHUNKS)],
                    held.at[pl.ds(start, source.shape[0])],
                    sems.at[len(copies)],
                )
            )
    for copy in copies:
        copy.start()
    marks[0] = jnp.ones((TILE, HEAD_DIM), jnp.bfloat16)
    marks[1] = jnp.zeros((TILE, HEAD_DIM), jnp.bfloat16)
    values[NO_TILE // CHUNKS] = jnp.zeros((CHUNKS, TILE, HEAD_DIM), jnp.bfloat16)
    for copy in copies[:4]:
        copy.wait()
    count = query.shape[0]

    def score_pair(row, tile_query, slot):
        ids = [slot_ids[0, slot + i, row] for i in range(2)]
        both = jnp.concatenate([keys[k >> 1, k & 1] for k in ids], axis=0)
        return lax.dot_general(
            tile_query, both, (((1,), (1,)), ((), ())), preferred_element_type=jnp.float32
        )

    def value_pair(row, slot):
        ids = [slot_ids[1, slot + i, row] for i in range(2)]
        return jnp.concatenate(
            [jnp.concatenate([values[k >> 1, k & 1], marks[k >> 7]], axis=1) for k in ids], axis=0
        )

    def fold(best, score):
        score = jnp.maximum(score[:, :TILE], score[:, TILE:])
        return score if best is None else jnp.maximum(best, score)

    def put_top(place, best):
        tops[place] = jnp.broadcast_to(jnp.max(best, axis=1, keepdims=True), (TILE, TILE))

    best = None
    for slot in range(0, KSEL, 2):
        score = score_pair(chunk, query[0], slot)
        scores[0, slot // 2] = score
        best = fold(best, score)
    put_top(0, best)
    for copy in copies[4:]:
        copy.wait()

    def step(turn, carry):
        for now in range(2):
            tile = turn * 2 + now
            later = jnp.minimum(tile + 1, count - 1)
            row, later_row = tile * CHUNKS + chunk, later * CHUNKS + chunk
            top = tops[now]
            top = jnp.concatenate([top, top], axis=1)
            later_query = query[later]
            best = None
            mixed = None
            for slot in range(0, KSEL, 2):
                score = score_pair(later_row, later_query, slot)
                scores[1 - now, slot // 2] = score
                best = fold(best, score)
                weights = jnp.exp2((scores[now, slot // 2] - top) * EXP2_SCALE)
                part = jnp.dot(
                    weights.astype(jnp.bfloat16),
                    value_pair(row, slot),
                    preferred_element_type=jnp.float32,
                )
                mixed = part if mixed is None else mixed + part
            put_top(1 - now, best)
            out_ref[tile] = (mixed[:, :HEAD_DIM] / mixed[:, HEAD_DIM:]).astype(jnp.bfloat16)
        return carry

    lax.fori_loop(0, count // 2, step, 0)


def attend(chunk, ids, query_tiles, left, own, right):
    count = query_tiles.shape[0]
    held = own.shape[0] + 2 * left.shape[0]
    whole = pl.BlockSpec(memory_space=pl.ANY)
    scalar = pl.BlockSpec(memory_space=pltpu.SMEM)
    return pl.pallas_call(
        functools.partial(attend_kernel, chunk),
        in_specs=[scalar, whole, whole, whole, whole],
        out_specs=pl.BlockSpec(memory_space=pltpu.VMEM),
        out_shape=jax.ShapeDtypeStruct((count, TILE, HEAD_DIM), jnp.bfloat16),
        scratch_shapes=[
            pltpu.VMEM((held, CHUNKS, TILE, HEAD_DIM), jnp.bfloat16),
            pltpu.VMEM((held + 1, CHUNKS, TILE, HEAD_DIM), jnp.bfloat16),
            pltpu.VMEM((count, TILE, HEAD_DIM), jnp.bfloat16),
            pltpu.VMEM((2, TILE, HEAD_DIM), jnp.bfloat16),
            pltpu.VMEM((2, KSEL // 2, TILE, 2 * TILE), jnp.float32),
            pltpu.VMEM((2, TILE, TILE), jnp.float32),
            pltpu.SemaphoreType.DMA((7,)),
        ],
        compiler_params=pltpu.CompilerParams(vmem_limit_bytes=60 * MIB),
        cost_estimate=pl.CostEstimate(
            flops=count * KSEL * TILE * TILE * HEAD_DIM * 4,
            bytes_accessed=12 * MIB,
            transcendentals=count * KSEL * TILE * TILE,
        ),
    )(ids, query_tiles, left, own, right)


def exchange(blocks):
    return lax.all_to_all(blocks, "seq", split_axis=0, concat_axis=0, tiled=True)


def per_device(queries, keys_values, extents, tile_lists):
    seq_size = lax.axis_size("seq")
    tm_size = lax.axis_size("tm")
    blocks, ids = split_pairs(keys_values, extents, tile_lists)
    first, second = split_queries(queries)
    own = exchange(blocks)
    half = seq_size // 2
    ends = tm_size - 1
    left = lax.ppermute(own[half:], "tm", [(i, i + 1) for i in range(ends)])
    right = lax.ppermute(own[:half], "tm", [(i + 1, i) for i in range(ends)])
    first = exchange(first)
    second = exchange(second)
    first_out = exchange(attend(0, ids, first, left, own, right))
    second_out = exchange(attend(1, ids, second, left, own, right))
    return join_heads(first_out, second_out)


def solution(mesh):
    placed = (P(("tm", "seq"), None), P(None, ("tm", "seq"), None), P(), P("tm", None))
    return jax.shard_map(
        per_device, mesh=mesh, in_specs=placed, out_specs=P(("tm", "seq"), None), check_vma=False
    )
```

```python
import functools

import jax
import jax.numpy as jnp
from jax import lax
from jax.experimental import pallas as pl
from jax.experimental.pallas import tpu as pltpu
from jax.sharding import PartitionSpec as P

HEAD_DIM = 128
TILE = 128
FRAME = 32
KSEL = 16
CHUNKS = 2
HEADS_STEP = 16
NO_TILE = 128
ALONG_X = 4
ALONG_Z = 8
EXP2_SCALE = HEAD_DIM ** (-0.5) * 1.4426950408889634
MIB = 1024 * 1024


def split_queries_kernel(query_ref, block_ref):
    for head in range(block_ref.shape[0]):
        columns = slice(head * HEAD_DIM, (head + 1) * HEAD_DIM)
        for chunk in range(CHUNKS):
            block_ref[head, chunk] = query_ref[chunk * TILE : (chunk + 1) * TILE, columns]


def split_queries(queries):
    tok_dev, width_all = queries.shape
    heads = width_all // HEAD_DIM
    return pl.pallas_call(
        split_queries_kernel,
        grid=(heads // HEADS_STEP,),
        in_specs=[pl.BlockSpec((tok_dev, HEADS_STEP * HEAD_DIM), lambda i: (0, i))],
        out_specs=pl.BlockSpec((HEADS_STEP, CHUNKS, TILE, HEAD_DIM), lambda i: (i, 0, 0, 0)),
        out_shape=jax.ShapeDtypeStruct((heads, CHUNKS, TILE, HEAD_DIM), jnp.bfloat16),
        compiler_params=pltpu.CompilerParams(vmem_limit_bytes=60 * MIB),
        cost_estimate=pl.CostEstimate(flops=0, bytes_accessed=4 * MIB, transcendentals=0),
    )(queries)


def split_pairs_kernel(extents, list_ref, pair_ref, block_ref, id_ref):
    for head in range(block_ref.shape[0]):
        columns = slice(head * HEAD_DIM, (head + 1) * HEAD_DIM)
        for part in range(2):
            for half in range(CHUNKS):
                rows = slice(half * TILE, (half + 1) * TILE)
                block_ref[head, part * CHUNKS + half] = pair_ref[part, rows, columns]

    @pl.when(pl.program_id(0) == 0)
    def _():
        head = lax.axis_index("seq")
        listed = list_ref[...]
        first = lax.axis_index("tm") * listed.shape[1]
        tiles = first + lax.broadcasted_iota(jnp.int32, listed.shape, 1)
        live = None
        for axis, (low, mask) in enumerate(((5, 15), (3, 3), (0, 7))):
            gap = jnp.abs(((listed >> low) & mask) - ((tiles >> low) & mask))
            near = gap <= extents[axis, head]
            live = near if live is None else live & near
        shift = first - FRAME
        id_ref[0] = jnp.where(live, listed, tiles) - shift
        id_ref[1] = jnp.where(live, listed - shift, NO_TILE)


def split_pairs(keys_values, extents, tile_lists):
    _, tok_dev, width_all = keys_values.shape
    heads = width_all // HEAD_DIM
    parts = 2 * CHUNKS
    rows, slots = tile_lists.shape
    return pl.pallas_call(
        split_pairs_kernel,
        grid=(heads // HEADS_STEP,),
        in_specs=[
            pl.BlockSpec(memory_space=pltpu.SMEM),
            pl.BlockSpec((slots, rows), lambda i: (0, 0)),
            pl.BlockSpec((2, tok_dev, HEADS_STEP * HEAD_DIM), lambda i: (0, 0, i)),
        ],
        out_specs=[
            pl.BlockSpec((HEADS_STEP, parts, TILE, HEAD_DIM), lambda i: (i, 0, 0, 0)),
            pl.BlockSpec((2, slots, rows), lambda i: (0, 0, 0)),
        ],
        out_shape=[
            jax.ShapeDtypeStruct((heads, parts, TILE, HEAD_DIM), jnp.bfloat16),
            jax.ShapeDtypeStruct((2, slots, rows), jnp.int32),
        ],
        compiler_params=pltpu.CompilerParams(vmem_limit_bytes=60 * MIB),
    )(extents, tile_lists.T, keys_values)


def join_kernel(first_hbm, second_hbm, out_hbm, held, in_sems, out_sems):
    sources = (first_hbm, second_hbm)
    reads = [
        [
            pltpu.make_async_copy(
                source.at[head],
                held.at[pl.ds(chunk * TILE, TILE), pl.ds(head * HEAD_DIM, HEAD_DIM)],
                in_sems.at[chunk, head],
            )
            for head in range(source.shape[0])
        ]
        for chunk, source in enumerate(sources)
    ]
    for copies in reads:
        for copy in copies:
            copy.start()
    writes = []
    for chunk, copies in enumerate(reads):
        for copy in copies:
            copy.wait()
        rows = pl.ds(chunk * TILE, TILE)
        writes.append(pltpu.make_async_copy(held.at[rows], out_hbm.at[rows], out_sems.at[chunk]))
        writes[-1].start()
    for copy in writes:
        copy.wait()


def join_heads(first, second):
    heads = first.shape[0]
    whole = pl.BlockSpec(memory_space=pl.ANY)
    shape = (CHUNKS * TILE, heads * HEAD_DIM)
    return pl.pallas_call(
        join_kernel,
        in_specs=[whole, whole],
        out_specs=whole,
        out_shape=jax.ShapeDtypeStruct(shape, jnp.bfloat16),
        scratch_shapes=[
            pltpu.VMEM(shape, jnp.bfloat16),
            pltpu.SemaphoreType.DMA((CHUNKS, heads)),
            pltpu.SemaphoreType.DMA((CHUNKS,)),
        ],
        compiler_params=pltpu.CompilerParams(vmem_limit_bytes=60 * MIB),
    )(first, second)


def attend_kernel(
    chunk,
    slot_ids,
    query_hbm,
    left_hbm,
    own_hbm,
    right_hbm,
    out_ref,
    keys,
    values,
    query,
    marks,
    scores,
    tops,
    sems,
):
    pairs = own_hbm.shape[0]
    rim = left_hbm.shape[0]
    places = ((own_hbm, rim), (left_hbm, 0), (right_hbm, rim + pairs))
    copies = [pltpu.make_async_copy(query_hbm, query, sems.at[0])]
    for part, held in enumerate((keys, values)):
        for source, start in places:
            copies.append(
                pltpu.make_async_copy(
                    source.at[:, pl.ds(part * CHUNKS, CHUNKS)],
                    held.at[pl.ds(start, source.shape[0])],
                    sems.at[len(copies)],
                )
            )
    for copy in copies:
        copy.start()
    marks[0] = jnp.ones((TILE, HEAD_DIM), jnp.bfloat16)
    marks[1] = jnp.zeros((TILE, HEAD_DIM), jnp.bfloat16)
    values[NO_TILE // CHUNKS] = jnp.zeros((CHUNKS, TILE, HEAD_DIM), jnp.bfloat16)
    for copy in copies[:4]:
        copy.wait()
    count = query.shape[0]
    here_x = lax.axis_index("seq") >> 3

    def pair_of(tile):
        return (((here_x - (tile & 3)) & 3) << 3) + (tile >> 2)

    def score_pair(row, tile_query, slot):
        ids = [slot_ids[0, slot + i, row] for i in range(2)]
        both = jnp.concatenate([keys[k >> 1, k & 1] for k in ids], axis=0)
        return lax.dot_general(
            tile_query, both, (((1,), (1,)), ((), ())), preferred_element_type=jnp.float32
        )

    def value_pair(row, slot):
        ids = [slot_ids[1, slot + i, row] for i in range(2)]
        return jnp.concatenate(
            [jnp.concatenate([values[k >> 1, k & 1], marks[k >> 7]], axis=1) for k in ids], axis=0
        )

    def fold(best, score):
        score = jnp.maximum(score[:, :TILE], score[:, TILE:])
        return score if best is None else jnp.maximum(best, score)

    def put_top(place, best):
        tops[place] = jnp.broadcast_to(jnp.max(best, axis=1, keepdims=True), (TILE, TILE))

    best = None
    first_row = pair_of(0) * CHUNKS + chunk
    for slot in range(0, KSEL, 2):
        score = score_pair(first_row, query[0], slot)
        scores[0, slot // 2] = score
        best = fold(best, score)
    put_top(0, best)
    for copy in copies[4:]:
        copy.wait()

    def step(turn, carry):
        for now in range(2):
            tile = turn * 2 + now
            later = jnp.minimum(tile + 1, count - 1)
            pair = pair_of(tile)
            row, later_row = pair * CHUNKS + chunk, pair_of(later) * CHUNKS + chunk
            top = tops[now]
            top = jnp.concatenate([top, top], axis=1)
            later_query = query[later]
            best = None
            mixed = None
            for slot in range(0, KSEL, 2):
                score = score_pair(later_row, later_query, slot)
                scores[1 - now, slot // 2] = score
                best = fold(best, score)
                weights = jnp.exp2((scores[now, slot // 2] - top) * EXP2_SCALE)
                part = jnp.dot(
                    weights.astype(jnp.bfloat16),
                    value_pair(row, slot),
                    preferred_element_type=jnp.float32,
                )
                mixed = part if mixed is None else mixed + part
            put_top(1 - now, best)
            out_ref[pair] = (mixed[:, :HEAD_DIM] / mixed[:, HEAD_DIM:]).astype(jnp.bfloat16)
        return carry

    lax.fori_loop(0, count // 2, step, 0)


def attend(chunk, ids, query_tiles, left, own, right):
    count = query_tiles.shape[0]
    held = own.shape[0] + 2 * left.shape[0]
    whole = pl.BlockSpec(memory_space=pl.ANY)
    scalar = pl.BlockSpec(memory_space=pltpu.SMEM)
    return pl.pallas_call(
        functools.partial(attend_kernel, chunk),
        in_specs=[scalar, whole, whole, whole, whole],
        out_specs=pl.BlockSpec(memory_space=pltpu.VMEM),
        out_shape=jax.ShapeDtypeStruct((count, TILE, HEAD_DIM), jnp.bfloat16),
        scratch_shapes=[
            pltpu.VMEM((held, CHUNKS, TILE, HEAD_DIM), jnp.bfloat16),
            pltpu.VMEM((held + 1, CHUNKS, TILE, HEAD_DIM), jnp.bfloat16),
            pltpu.VMEM((count, TILE, HEAD_DIM), jnp.bfloat16),
            pltpu.VMEM((2, TILE, HEAD_DIM), jnp.bfloat16),
            pltpu.VMEM((2, KSEL // 2, TILE, 2 * TILE), jnp.float32),
            pltpu.VMEM((2, TILE, TILE), jnp.float32),
            pltpu.SemaphoreType.DMA((7,)),
        ],
        compiler_params=pltpu.CompilerParams(vmem_limit_bytes=60 * MIB),
        cost_estimate=pl.CostEstimate(
            flops=count * KSEL * TILE * TILE * HEAD_DIM * 4,
            bytes_accessed=12 * MIB,
            transcendentals=count * KSEL * TILE * TILE,
        ),
    )(ids, query_tiles, left, own, right)


def exchange(blocks):
    return lax.all_to_all(blocks, "seq", split_axis=0, concat_axis=0, tiled=True)


def exchange_z(blocks):
    groups = [[x * ALONG_Z + z for z in range(ALONG_Z)] for x in range(ALONG_X)]
    return lax.all_to_all(
        blocks, "seq", split_axis=0, concat_axis=0, tiled=True, axis_index_groups=groups
    )


def shift_x(blocks, by):
    pairs = [
        (x * ALONG_Z + z, (x + by) % ALONG_X * ALONG_Z + z)
        for x in range(ALONG_X)
        for z in range(ALONG_Z)
    ]
    return lax.ppermute(blocks, "seq", pairs)


def queries_by_x(queries):
    blocks = split_queries(queries)
    x = lax.axis_index("seq") // ALONG_Z
    parts = []
    for by in range(ALONG_X):
        start = (x + by) % ALONG_X * ALONG_Z
        part = lax.dynamic_slice_in_dim(blocks, start, ALONG_Z, axis=0)
        parts.append(shift_x(part, by) if by else part)
    return [
        jnp.stack([part[:, chunk] for part in parts], axis=1).reshape(-1, TILE, HEAD_DIM)
        for chunk in range(CHUNKS)
    ]


def per_device(queries, keys_values, extents, tile_lists):
    seq_size = lax.axis_size("seq")
    tm_size = lax.axis_size("tm")
    blocks, ids = split_pairs(keys_values, extents, tile_lists)
    first, second = queries_by_x(queries)
    own = exchange(blocks)
    half = seq_size // 2
    ends = tm_size - 1
    left = lax.ppermute(own[half:], "tm", [(i, i + 1) for i in range(ends)])
    right = lax.ppermute(own[:half], "tm", [(i + 1, i) for i in range(ends)])
    first = exchange_z(first)
    second = exchange_z(second)
    first_out = exchange(attend(0, ids, first, left, own, right))
    second_out = exchange(attend(1, ids, second, left, own, right))
    return join_heads(first_out, second_out)


def solution(mesh):
    placed = (P(("tm", "seq"), None), P(None, ("tm", "seq"), None), P(), P("tm", None))
    return jax.shard_map(
        per_device, mesh=mesh, in_specs=placed, out_specs=P(("tm", "seq"), None), check_vma=False
    )
```

```python
import functools

import jax
import jax.numpy as jnp
from jax import lax
from jax.experimental import pallas as pl
from jax.experimental.pallas import tpu as pltpu
from jax.sharding import PartitionSpec as P

HEAD_DIM = 128
TILE = 128
FRAME = 32
KSEL = 16
CHUNKS = 2
HEADS_STEP = 16
NO_TILE = 128
ALONG_X = 4
ALONG_Z = 8
EXP2_SCALE = HEAD_DIM ** (-0.5) * 1.4426950408889634
MIB = 1024 * 1024


def split_queries_kernel(query_ref, block_ref):
    for head in range(block_ref.shape[0]):
        columns = slice(head * HEAD_DIM, (head + 1) * HEAD_DIM)
        for chunk in range(CHUNKS):
            block_ref[head, chunk] = query_ref[chunk * TILE : (chunk + 1) * TILE, columns]


def split_queries(queries):
    tok_dev, width_all = queries.shape
    heads = width_all // HEAD_DIM
    return pl.pallas_call(
        split_queries_kernel,
        grid=(heads // HEADS_STEP,),
        in_specs=[pl.BlockSpec((tok_dev, HEADS_STEP * HEAD_DIM), lambda i: (0, i))],
        out_specs=pl.BlockSpec((HEADS_STEP, CHUNKS, TILE, HEAD_DIM), lambda i: (i, 0, 0, 0)),
        out_shape=jax.ShapeDtypeStruct((heads, CHUNKS, TILE, HEAD_DIM), jnp.bfloat16),
        compiler_params=pltpu.CompilerParams(vmem_limit_bytes=60 * MIB),
        cost_estimate=pl.CostEstimate(flops=0, bytes_accessed=4 * MIB, transcendentals=0),
    )(queries)


def split_pairs_kernel(extents, list_ref, pair_ref, block_ref, id_ref):
    for head in range(block_ref.shape[0]):
        columns = slice(head * HEAD_DIM, (head + 1) * HEAD_DIM)
        for part in range(2):
            for half in range(CHUNKS):
                rows = slice(half * TILE, (half + 1) * TILE)
                block_ref[head, part * CHUNKS + half] = pair_ref[part, rows, columns]

    @pl.when(pl.program_id(0) == 0)
    def _():
        head = lax.axis_index("seq")
        listed = list_ref[...]
        first = lax.axis_index("tm") * listed.shape[1]
        tiles = first + lax.broadcasted_iota(jnp.int32, listed.shape, 1)
        live = None
        for axis, (low, mask) in enumerate(((5, 15), (3, 3), (0, 7))):
            gap = jnp.abs(((listed >> low) & mask) - ((tiles >> low) & mask))
            near = gap <= extents[axis, head]
            live = near if live is None else live & near
        shift = first - FRAME
        id_ref[0] = jnp.where(live, listed, tiles) - shift
        id_ref[1] = jnp.where(live, listed - shift, NO_TILE)


def split_pairs(keys_values, extents, tile_lists):
    _, tok_dev, width_all = keys_values.shape
    heads = width_all // HEAD_DIM
    parts = 2 * CHUNKS
    rows, slots = tile_lists.shape
    return pl.pallas_call(
        split_pairs_kernel,
        grid=(heads // HEADS_STEP,),
        in_specs=[
            pl.BlockSpec(memory_space=pltpu.SMEM),
            pl.BlockSpec((slots, rows), lambda i: (0, 0)),
            pl.BlockSpec((2, tok_dev, HEADS_STEP * HEAD_DIM), lambda i: (0, 0, i)),
        ],
        out_specs=[
            pl.BlockSpec((HEADS_STEP, parts, TILE, HEAD_DIM), lambda i: (i, 0, 0, 0)),
            pl.BlockSpec((2, slots, rows), lambda i: (0, 0, 0)),
        ],
        out_shape=[
            jax.ShapeDtypeStruct((heads, parts, TILE, HEAD_DIM), jnp.bfloat16),
            jax.ShapeDtypeStruct((2, slots, rows), jnp.int32),
        ],
        compiler_params=pltpu.CompilerParams(vmem_limit_bytes=60 * MIB),
    )(extents, tile_lists.T, keys_values)


def join_kernel(chunk, source_hbm, *refs):
    out_hbm, held, in_sems, out_sem = refs[-4:]
    reads = [
        pltpu.make_async_copy(
            source_hbm.at[head], held.at[:, pl.ds(head * HEAD_DIM, HEAD_DIM)], in_sems.at[head]
        )
        for head in range(source_hbm.shape[0])
    ]
    for copy in reads:
        copy.start()
    for copy in reads:
        copy.wait()
    write = pltpu.make_async_copy(held, out_hbm.at[pl.ds(chunk * TILE, TILE)], out_sem)
    write.start()
    write.wait()


def join_heads(chunk, source, *joined):
    heads = source.shape[0]
    width = heads * HEAD_DIM
    whole = pl.BlockSpec(memory_space=pl.ANY)
    return pl.pallas_call(
        functools.partial(join_kernel, chunk),
        in_specs=[whole] * (1 + len(joined)),
        out_specs=whole,
        out_shape=jax.ShapeDtypeStruct((CHUNKS * TILE, width), jnp.bfloat16),
        input_output_aliases={1: 0} if joined else {},
        scratch_shapes=[
            pltpu.VMEM((TILE, width), jnp.bfloat16),
            pltpu.SemaphoreType.DMA((heads,)),
            pltpu.SemaphoreType.DMA,
        ],
        compiler_params=pltpu.CompilerParams(vmem_limit_bytes=8 * MIB),
        cost_estimate=pl.CostEstimate(flops=0, bytes_accessed=4 * MIB, transcendentals=0),
    )(source, *joined)


def attend_kernel(
    chunk,
    slot_ids,
    query_hbm,
    left_hbm,
    own_hbm,
    right_hbm,
    out_ref,
    keys,
    values,
    query,
    marks,
    scores,
    tops,
    sems,
):
    pairs = own_hbm.shape[0]
    rim = left_hbm.shape[0]
    places = ((own_hbm, rim), (left_hbm, 0), (right_hbm, rim + pairs))
    copies = [pltpu.make_async_copy(query_hbm, query, sems.at[0])]
    for part, held in enumerate((keys, values)):
        for source, start in places:
            copies.append(
                pltpu.make_async_copy(
                    source.at[:, pl.ds(part * CHUNKS, CHUNKS)],
                    held.at[pl.ds(start, source.shape[0])],
                    sems.at[len(copies)],
                )
            )
    for copy in copies:
        copy.start()
    marks[0] = jnp.ones((TILE, HEAD_DIM), jnp.bfloat16)
    marks[1] = jnp.zeros((TILE, HEAD_DIM), jnp.bfloat16)
    values[NO_TILE // CHUNKS] = jnp.zeros((CHUNKS, TILE, HEAD_DIM), jnp.bfloat16)
    for copy in copies[:4]:
        copy.wait()
    count = query.shape[0]
    here_x = lax.axis_index("seq") >> 3

    def pair_of(tile):
        return (((here_x - (tile & 3)) & 3) << 3) + (tile >> 2)

    def score_pair(row, tile_query, slot):
        ids = [slot_ids[0, slot + i, row] for i in range(2)]
        both = jnp.concatenate([keys[k >> 1, k & 1] for k in ids], axis=0)
        return lax.dot_general(
            tile_query, both, (((1,), (1,)), ((), ())), preferred_element_type=jnp.float32
        )

    def value_pair(row, slot):
        ids = [slot_ids[1, slot + i, row] for i in range(2)]
        return jnp.concatenate(
            [jnp.concatenate([values[k >> 1, k & 1], marks[k >> 7]], axis=1) for k in ids], axis=0
        )

    def fold(best, score):
        score = jnp.maximum(score[:, :TILE], score[:, TILE:])
        return score if best is None else jnp.maximum(best, score)

    def put_top(place, best):
        tops[place] = jnp.broadcast_to(jnp.max(best, axis=1, keepdims=True), (TILE, TILE))

    best = None
    first_row = pair_of(0) * CHUNKS + chunk
    for slot in range(0, KSEL, 2):
        score = score_pair(first_row, query[0], slot)
        scores[0, slot // 2] = score
        best = fold(best, score)
    put_top(0, best)
    for copy in copies[4:]:
        copy.wait()

    def step(turn, carry):
        for now in range(2):
            tile = turn * 2 + now
            later = jnp.minimum(tile + 1, count - 1)
            pair = pair_of(tile)
            row, later_row = pair * CHUNKS + chunk, pair_of(later) * CHUNKS + chunk
            top = tops[now]
            top = jnp.concatenate([top, top], axis=1)
            later_query = query[later]
            best = None
            mixed = None
            for slot in range(0, KSEL, 2):
                score = score_pair(later_row, later_query, slot)
                scores[1 - now, slot // 2] = score
                best = fold(best, score)
                weights = jnp.exp2((scores[now, slot // 2] - top) * EXP2_SCALE)
                part = jnp.dot(
                    weights.astype(jnp.bfloat16),
                    value_pair(row, slot),
                    preferred_element_type=jnp.float32,
                )
                mixed = part if mixed is None else mixed + part
            put_top(1 - now, best)
            out_ref[pair] = (mixed[:, :HEAD_DIM] / mixed[:, HEAD_DIM:]).astype(jnp.bfloat16)
        return carry

    lax.fori_loop(0, count // 2, step, 0)


def attend(chunk, ids, query_tiles, left, own, right):
    count = query_tiles.shape[0]
    held = own.shape[0] + 2 * left.shape[0]
    whole = pl.BlockSpec(memory_space=pl.ANY)
    scalar = pl.BlockSpec(memory_space=pltpu.SMEM)
    return pl.pallas_call(
        functools.partial(attend_kernel, chunk),
        in_specs=[scalar, whole, whole, whole, whole],
        out_specs=pl.BlockSpec(memory_space=pltpu.VMEM),
        out_shape=jax.ShapeDtypeStruct((count, TILE, HEAD_DIM), jnp.bfloat16),
        scratch_shapes=[
            pltpu.VMEM((held, CHUNKS, TILE, HEAD_DIM), jnp.bfloat16),
            pltpu.VMEM((held + 1, CHUNKS, TILE, HEAD_DIM), jnp.bfloat16),
            pltpu.VMEM((count, TILE, HEAD_DIM), jnp.bfloat16),
            pltpu.VMEM((2, TILE, HEAD_DIM), jnp.bfloat16),
            pltpu.VMEM((2, KSEL // 2, TILE, 2 * TILE), jnp.float32),
            pltpu.VMEM((2, TILE, TILE), jnp.float32),
            pltpu.SemaphoreType.DMA((7,)),
        ],
        compiler_params=pltpu.CompilerParams(vmem_limit_bytes=16 * MIB),
        cost_estimate=pl.CostEstimate(
            flops=count * KSEL * TILE * TILE * HEAD_DIM * 4,
            bytes_accessed=12 * MIB,
            transcendentals=count * KSEL * TILE * TILE,
        ),
    )(ids, query_tiles, left, own, right)


def exchange(blocks):
    return lax.all_to_all(blocks, "seq", split_axis=0, concat_axis=0, tiled=True)


def exchange_z(blocks):
    groups = [[x * ALONG_Z + z for z in range(ALONG_Z)] for x in range(ALONG_X)]
    return lax.all_to_all(
        blocks, "seq", split_axis=0, concat_axis=0, tiled=True, axis_index_groups=groups
    )


def shift_x(blocks, by):
    pairs = [
        (x * ALONG_Z + z, (x + by) % ALONG_X * ALONG_Z + z)
        for x in range(ALONG_X)
        for z in range(ALONG_Z)
    ]
    return lax.ppermute(blocks, "seq", pairs)


def queries_by_x(queries):
    blocks = split_queries(queries)
    x = lax.axis_index("seq") // ALONG_Z
    parts = []
    for by in range(ALONG_X):
        start = (x + by) % ALONG_X * ALONG_Z
        part = lax.dynamic_slice_in_dim(blocks, start, ALONG_Z, axis=0)
        parts.append(shift_x(part, by) if by else part)
    return [
        jnp.stack([part[:, chunk] for part in parts], axis=1).reshape(-1, TILE, HEAD_DIM)
        for chunk in range(CHUNKS)
    ]


def per_device(queries, keys_values, extents, tile_lists):
    seq_size = lax.axis_size("seq")
    tm_size = lax.axis_size("tm")
    blocks, ids = split_pairs(keys_values, extents, tile_lists)
    first, second = queries_by_x(queries)
    own = exchange(blocks)
    half = seq_size // 2
    ends = tm_size - 1
    left = lax.ppermute(own[half:], "tm", [(i, i + 1) for i in range(ends)])
    right = lax.ppermute(own[:half], "tm", [(i + 1, i) for i in range(ends)])
    first = exchange_z(first)
    second = exchange_z(second)
    first_out = exchange(attend(0, ids, first, left, own, right))
    second_out = exchange(attend(1, ids, second, left, own, right))
    return join_heads(1, second_out, join_heads(0, first_out))


def solution(mesh):
    placed = (P(("tm", "seq"), None), P(None, ("tm", "seq"), None), P(), P("tm", None))
    return jax.shard_map(
        per_device, mesh=mesh, in_specs=placed, out_specs=P(("tm", "seq"), None), check_vma=False
    )
```

```python
import functools

import jax
import jax.numpy as jnp
from jax import lax
from jax.experimental import pallas as pl
from jax.experimental.pallas import tpu as pltpu
from jax.sharding import PartitionSpec as P

HEAD_DIM = 128
TILE = 128
FRAME = 32
KSEL = 16
CHUNKS = 2
HEADS_STEP = 16
NO_TILE = 128
ALONG_X = 4
ALONG_Z = 8
EXP2_SCALE = HEAD_DIM ** (-0.5) * 1.4426950408889634
MIB = 1024 * 1024


def split_queries_kernel(query_ref, block_ref):
    for head in range(block_ref.shape[0]):
        columns = slice(head * HEAD_DIM, (head + 1) * HEAD_DIM)
        for chunk in range(CHUNKS):
            block_ref[head, chunk] = query_ref[chunk * TILE : (chunk + 1) * TILE, columns]


def split_queries(queries):
    tok_dev, width_all = queries.shape
    heads = width_all // HEAD_DIM
    return pl.pallas_call(
        split_queries_kernel,
        grid=(heads // HEADS_STEP,),
        in_specs=[pl.BlockSpec((tok_dev, HEADS_STEP * HEAD_DIM), lambda i: (0, i))],
        out_specs=pl.BlockSpec((HEADS_STEP, CHUNKS, TILE, HEAD_DIM), lambda i: (i, 0, 0, 0)),
        out_shape=jax.ShapeDtypeStruct((heads, CHUNKS, TILE, HEAD_DIM), jnp.bfloat16),
        compiler_params=pltpu.CompilerParams(vmem_limit_bytes=60 * MIB),
        cost_estimate=pl.CostEstimate(flops=0, bytes_accessed=4 * MIB, transcendentals=0),
    )(queries)


def split_pairs_kernel(extents, list_ref, pair_ref, block_ref, id_ref):
    for head in range(block_ref.shape[0]):
        columns = slice(head * HEAD_DIM, (head + 1) * HEAD_DIM)
        for part in range(2):
            for half in range(CHUNKS):
                rows = slice(half * TILE, (half + 1) * TILE)
                block_ref[head, part * CHUNKS + half] = pair_ref[part, rows, columns]

    @pl.when(pl.program_id(0) == 0)
    def _():
        head = lax.axis_index("seq")
        listed = list_ref[...]
        first = lax.axis_index("tm") * listed.shape[1]
        tiles = first + lax.broadcasted_iota(jnp.int32, listed.shape, 1)
        live = None
        for axis, (low, mask) in enumerate(((5, 15), (3, 3), (0, 7))):
            gap = jnp.abs(((listed >> low) & mask) - ((tiles >> low) & mask))
            near = gap <= extents[axis, head]
            live = near if live is None else live & near
        shift = first - FRAME
        id_ref[0] = jnp.where(live, listed, tiles) - shift
        id_ref[1] = jnp.where(live, listed - shift, NO_TILE)


def split_pairs(keys_values, extents, tile_lists):
    _, tok_dev, width_all = keys_values.shape
    heads = width_all // HEAD_DIM
    parts = 2 * CHUNKS
    rows, slots = tile_lists.shape
    return pl.pallas_call(
        split_pairs_kernel,
        grid=(heads // HEADS_STEP,),
        in_specs=[
            pl.BlockSpec(memory_space=pltpu.SMEM),
            pl.BlockSpec((slots, rows), lambda i: (0, 0)),
            pl.BlockSpec((2, tok_dev, HEADS_STEP * HEAD_DIM), lambda i: (0, 0, i)),
        ],
        out_specs=[
            pl.BlockSpec((HEADS_STEP, parts, TILE, HEAD_DIM), lambda i: (i, 0, 0, 0)),
            pl.BlockSpec((2, slots, rows), lambda i: (0, 0, 0)),
        ],
        out_shape=[
            jax.ShapeDtypeStruct((heads, parts, TILE, HEAD_DIM), jnp.bfloat16),
            jax.ShapeDtypeStruct((2, slots, rows), jnp.int32),
        ],
        compiler_params=pltpu.CompilerParams(vmem_limit_bytes=60 * MIB),
    )(extents, tile_lists.T, keys_values)


def join_kernel(chunk, count, *refs):
    sources, (out_hbm, held, in_sems, out_sem) = refs[:count], refs[-4:]
    here_x = lax.axis_index("seq") >> 3
    reads = []
    for by, source_hbm in enumerate(sources):
        for place in range(source_hbm.shape[0]):
            head = place if count == 1 else ((here_x + by) & 3) * ALONG_Z + place
            columns = pl.ds(pl.multiple_of(head * HEAD_DIM, HEAD_DIM), HEAD_DIM)
            reads.append(
                pltpu.make_async_copy(
                    source_hbm.at[place], held.at[:, columns], in_sems.at[len(reads)]
                )
            )
    for copy in reads:
        copy.start()
    for copy in reads:
        copy.wait()
    write = pltpu.make_async_copy(held, out_hbm.at[pl.ds(chunk * TILE, TILE)], out_sem)
    write.start()
    write.wait()


def join_heads(chunk, sources, *joined):
    heads = sum(source.shape[0] for source in sources)
    width = heads * HEAD_DIM
    whole = pl.BlockSpec(memory_space=pl.ANY)
    return pl.pallas_call(
        functools.partial(join_kernel, chunk, len(sources)),
        in_specs=[whole] * (len(sources) + len(joined)),
        out_specs=whole,
        out_shape=jax.ShapeDtypeStruct((CHUNKS * TILE, width), jnp.bfloat16),
        input_output_aliases={len(sources): 0} if joined else {},
        scratch_shapes=[
            pltpu.VMEM((TILE, width), jnp.bfloat16),
            pltpu.SemaphoreType.DMA((heads,)),
            pltpu.SemaphoreType.DMA,
        ],
        compiler_params=pltpu.CompilerParams(vmem_limit_bytes=8 * MIB),
        cost_estimate=pl.CostEstimate(flops=0, bytes_accessed=4 * MIB, transcendentals=0),
    )(*sources, *joined)


def attend_kernel(
    chunk,
    slot_ids,
    query_hbm,
    left_hbm,
    own_hbm,
    right_hbm,
    out_ref,
    keys,
    values,
    query,
    marks,
    scores,
    tops,
    sems,
):
    pairs = own_hbm.shape[0]
    rim = left_hbm.shape[0]
    places = ((own_hbm, rim), (left_hbm, 0), (right_hbm, rim + pairs))
    copies = [pltpu.make_async_copy(query_hbm, query, sems.at[0])]
    for part, held in enumerate((keys, values)):
        for source, start in places:
            copies.append(
                pltpu.make_async_copy(
                    source.at[:, pl.ds(part * CHUNKS, CHUNKS)],
                    held.at[pl.ds(start, source.shape[0])],
                    sems.at[len(copies)],
                )
            )
    for copy in copies:
        copy.start()
    marks[0] = jnp.ones((TILE, HEAD_DIM), jnp.bfloat16)
    marks[1] = jnp.zeros((TILE, HEAD_DIM), jnp.bfloat16)
    values[NO_TILE // CHUNKS] = jnp.zeros((CHUNKS, TILE, HEAD_DIM), jnp.bfloat16)
    for copy in copies[:4]:
        copy.wait()
    count = query.shape[0]
    here_x = lax.axis_index("seq") >> 3

    def pair_of(tile):
        return (((here_x - (tile & 3)) & 3) << 3) + (tile >> 2)

    def score_pair(row, tile_query, slot):
        ids = [slot_ids[0, slot + i, row] for i in range(2)]
        both = jnp.concatenate([keys[k >> 1, k & 1] for k in ids], axis=0)
        return lax.dot_general(
            tile_query, both, (((1,), (1,)), ((), ())), preferred_element_type=jnp.float32
        )

    def value_pair(row, slot):
        ids = [slot_ids[1, slot + i, row] for i in range(2)]
        return jnp.concatenate(
            [jnp.concatenate([values[k >> 1, k & 1], marks[k >> 7]], axis=1) for k in ids], axis=0
        )

    def fold(best, score):
        score = jnp.maximum(score[:, :TILE], score[:, TILE:])
        return score if best is None else jnp.maximum(best, score)

    def put_top(place, best):
        tops[place] = jnp.broadcast_to(jnp.max(best, axis=1, keepdims=True), (TILE, TILE))

    best = None
    first_row = pair_of(0) * CHUNKS + chunk
    for slot in range(0, KSEL, 2):
        score = score_pair(first_row, query[0], slot)
        scores[0, slot // 2] = score
        best = fold(best, score)
    put_top(0, best)
    for copy in copies[4:]:
        copy.wait()

    def step(turn, carry):
        for now in range(2):
            tile = turn * 2 + now
            later = jnp.minimum(tile + 1, count - 1)
            pair = pair_of(tile)
            row, later_row = pair * CHUNKS + chunk, pair_of(later) * CHUNKS + chunk
            top = tops[now]
            top = jnp.concatenate([top, top], axis=1)
            later_query = query[later]
            best = None
            mixed = None
            for slot in range(0, KSEL, 2):
                score = score_pair(later_row, later_query, slot)
                scores[1 - now, slot // 2] = score
                best = fold(best, score)
                weights = jnp.exp2((scores[now, slot // 2] - top) * EXP2_SCALE)
                part = jnp.dot(
                    weights.astype(jnp.bfloat16),
                    value_pair(row, slot),
                    preferred_element_type=jnp.float32,
                )
                mixed = part if mixed is None else mixed + part
            put_top(1 - now, best)
            out_ref[tile if chunk == 0 else pair] = (mixed[:, :HEAD_DIM] / mixed[:, HEAD_DIM:]).astype(jnp.bfloat16)
        return carry

    lax.fori_loop(0, count // 2, step, 0)


def attend(chunk, ids, query_tiles, left, own, right):
    count = query_tiles.shape[0]
    held = own.shape[0] + 2 * left.shape[0]
    whole = pl.BlockSpec(memory_space=pl.ANY)
    scalar = pl.BlockSpec(memory_space=pltpu.SMEM)
    return pl.pallas_call(
        functools.partial(attend_kernel, chunk),
        in_specs=[scalar, whole, whole, whole, whole],
        out_specs=pl.BlockSpec(memory_space=pltpu.VMEM),
        out_shape=jax.ShapeDtypeStruct((count, TILE, HEAD_DIM), jnp.bfloat16),
        scratch_shapes=[
            pltpu.VMEM((held, CHUNKS, TILE, HEAD_DIM), jnp.bfloat16),
            pltpu.VMEM((held + 1, CHUNKS, TILE, HEAD_DIM), jnp.bfloat16),
            pltpu.VMEM((count, TILE, HEAD_DIM), jnp.bfloat16),
            pltpu.VMEM((2, TILE, HEAD_DIM), jnp.bfloat16),
            pltpu.VMEM((2, KSEL // 2, TILE, 2 * TILE), jnp.float32),
            pltpu.VMEM((2, TILE, TILE), jnp.float32),
            pltpu.SemaphoreType.DMA((7,)),
        ],
        compiler_params=pltpu.CompilerParams(vmem_limit_bytes=16 * MIB),
        cost_estimate=pl.CostEstimate(
            flops=count * KSEL * TILE * TILE * HEAD_DIM * 4,
            bytes_accessed=12 * MIB,
            transcendentals=count * KSEL * TILE * TILE,
        ),
    )(ids, query_tiles, left, own, right)


def exchange(blocks):
    return lax.all_to_all(blocks, "seq", split_axis=0, concat_axis=0, tiled=True)


def exchange_z(blocks):
    groups = [[x * ALONG_Z + z for z in range(ALONG_Z)] for x in range(ALONG_X)]
    return lax.all_to_all(
        blocks, "seq", split_axis=0, concat_axis=0, tiled=True, axis_index_groups=groups
    )


def shift_x(blocks, by):
    pairs = [
        (x * ALONG_Z + z, (x + by) % ALONG_X * ALONG_Z + z)
        for x in range(ALONG_X)
        for z in range(ALONG_Z)
    ]
    return lax.ppermute(blocks, "seq", pairs)


def queries_by_x(queries):
    blocks = split_queries(queries)
    x = lax.axis_index("seq") // ALONG_Z
    parts = []
    for by in range(ALONG_X):
        start = (x + by) % ALONG_X * ALONG_Z
        part = lax.dynamic_slice_in_dim(blocks, start, ALONG_Z, axis=0)
        parts.append(shift_x(part, by) if by else part)
    return [
        jnp.stack([part[:, chunk] for part in parts], axis=1).reshape(-1, TILE, HEAD_DIM)
        for chunk in range(CHUNKS)
    ]


def outputs_by_x(blocks):
    blocks = blocks.reshape(ALONG_Z, ALONG_X, TILE, HEAD_DIM)
    return [
        shift_x(blocks[:, by], ALONG_X - by) if by else blocks[:, by] for by in range(ALONG_X)
    ]


def per_device(queries, keys_values, extents, tile_lists):
    seq_size = lax.axis_size("seq")
    tm_size = lax.axis_size("tm")
    blocks, ids = split_pairs(keys_values, extents, tile_lists)
    first, second = queries_by_x(queries)
    own = exchange(blocks)
    half = seq_size // 2
    ends = tm_size - 1
    left = lax.ppermute(own[half:], "tm", [(i, i + 1) for i in range(ends)])
    right = lax.ppermute(own[:half], "tm", [(i + 1, i) for i in range(ends)])
    first = exchange_z(first)
    second = exchange_z(second)
    first_out = exchange_z(attend(0, ids, first, left, own, right))
    first_out = outputs_by_x(first_out)
    second_out = exchange(attend(1, ids, second, left, own, right))
    return join_heads(1, [second_out], join_heads(0, first_out))


def solution(mesh):
    placed = (P(("tm", "seq"), None), P(None, ("tm", "seq"), None), P(), P("tm", None))
    return jax.shard_map(
        per_device, mesh=mesh, in_specs=placed, out_specs=P(("tm", "seq"), None), check_vma=False
    )
```

```python
import functools

import jax
import jax.numpy as jnp
from jax import lax
from jax.experimental import pallas as pl
from jax.experimental.pallas import tpu as pltpu
from jax.sharding import PartitionSpec as P

HEAD_DIM = 128
TILE = 128
FRAME = 32
KSEL = 16
CHUNKS = 2
HEADS_STEP = 16
NO_TILE = 128
ALONG_X = 4
PIECE = 32
ALONG_Z = 8
EXP2_SCALE = HEAD_DIM ** (-0.5) * 1.4426950408889634
MIB = 1024 * 1024


def split_queries_kernel(query_ref, block_ref):
    for head in range(block_ref.shape[0]):
        columns = slice(head * HEAD_DIM, (head + 1) * HEAD_DIM)
        for chunk in range(CHUNKS):
            block_ref[head, chunk] = query_ref[chunk * TILE : (chunk + 1) * TILE, columns]


def split_queries(queries):
    tok_dev, width_all = queries.shape
    heads = width_all // HEAD_DIM
    return pl.pallas_call(
        split_queries_kernel,
        grid=(heads // HEADS_STEP,),
        in_specs=[pl.BlockSpec((tok_dev, HEADS_STEP * HEAD_DIM), lambda i: (0, i))],
        out_specs=pl.BlockSpec((HEADS_STEP, CHUNKS, TILE, HEAD_DIM), lambda i: (i, 0, 0, 0)),
        out_shape=jax.ShapeDtypeStruct((heads, CHUNKS, TILE, HEAD_DIM), jnp.bfloat16),
        compiler_params=pltpu.CompilerParams(vmem_limit_bytes=60 * MIB),
        cost_estimate=pl.CostEstimate(flops=0, bytes_accessed=4 * MIB, transcendentals=0),
    )(queries)


def split_pairs_kernel(extents, list_ref, pair_hbm, block_hbm, id_ref, rows_in, rows_out, sems):
    pieces = TILE // PIECE
    reads, writes = [], []
    for part in range(2):
        for piece in range(CHUNKS * pieces):
            place = len(reads)
            rows = pl.ds(piece * PIECE, PIECE)
            reads.append(
                pltpu.make_async_copy(pair_hbm.at[part, rows], rows_in.at[place], sems.at[0, place])
            )
            block = part * CHUNKS + piece // pieces
            rows = pl.ds(piece % pieces * PIECE, PIECE)
            writes.append(
                pltpu.make_async_copy(
                    rows_out.at[place], block_hbm.at[:, block, rows], sems.at[1, place]
                )
            )
    for copy in reads:
        copy.start()

    here = lax.axis_index("seq")
    listed = list_ref[...]
    first = lax.axis_index("tm") * listed.shape[1]
    tiles = first + lax.broadcasted_iota(jnp.int32, listed.shape, 1)
    live = None
    for axis, (low, mask) in enumerate(((5, 15), (3, 3), (0, 7))):
        gap = jnp.abs(((listed >> low) & mask) - ((tiles >> low) & mask))
        near = gap <= extents[axis, here]
        live = near if live is None else live & near
    shift = first - FRAME
    id_ref[0] = jnp.where(live, listed, tiles) - shift
    id_ref[1] = jnp.where(live, listed - shift, NO_TILE)

    for place, (read, write) in enumerate(zip(reads, writes)):
        read.wait()
        for head in range(rows_out.shape[1]):
            rows_out[place, head] = rows_in[place, :, head * HEAD_DIM : (head + 1) * HEAD_DIM]
        write.start()
    for copy in writes:
        copy.wait()


def split_pairs(keys_values, extents, tile_lists):
    _, tok_dev, width_all = keys_values.shape
    heads = width_all // HEAD_DIM
    places = 2 * tok_dev // PIECE
    rows, slots = tile_lists.shape
    whole = pl.BlockSpec(memory_space=pl.ANY)
    local = pl.BlockSpec(memory_space=pltpu.VMEM)
    return pl.pallas_call(
        split_pairs_kernel,
        in_specs=[pl.BlockSpec(memory_space=pltpu.SMEM), local, whole],
        out_specs=[whole, local],
        out_shape=[
            jax.ShapeDtypeStruct((heads, 2 * CHUNKS, TILE, HEAD_DIM), jnp.bfloat16),
            jax.ShapeDtypeStruct((2, slots, rows), jnp.int32),
        ],
        scratch_shapes=[
            pltpu.VMEM((places, PIECE, width_all), jnp.bfloat16),
            pltpu.VMEM((places, heads, PIECE, HEAD_DIM), jnp.bfloat16),
            pltpu.SemaphoreType.DMA((2, places)),
        ],
        compiler_params=pltpu.CompilerParams(vmem_limit_bytes=60 * MIB),
    )(extents, tile_lists.T, keys_values)


def join_kernel(chunk, count, *refs):
    sources, (out_hbm, held, in_sems, out_sem) = refs[:count], refs[-4:]
    here_x = lax.axis_index("seq") >> 3
    reads = []
    for by, source_hbm in enumerate(sources):
        for place in range(source_hbm.shape[0]):
            if count == 1:
                head = ((here_x - (place & 3)) & 3) * ALONG_Z + (place >> 2)
            else:
                head = ((here_x + by) & 3) * ALONG_Z + place
            columns = pl.ds(pl.multiple_of(head * HEAD_DIM, HEAD_DIM), HEAD_DIM)
            reads.append(
                pltpu.make_async_copy(
                    source_hbm.at[place], held.at[:, columns], in_sems.at[len(reads)]
                )
            )
    for copy in reads:
        copy.start()
    for copy in reads:
        copy.wait()
    write = pltpu.make_async_copy(held, out_hbm.at[pl.ds(chunk * TILE, TILE)], out_sem)
    write.start()
    write.wait()


def join_heads(chunk, sources, *joined):
    heads = sum(source.shape[0] for source in sources)
    width = heads * HEAD_DIM
    whole = pl.BlockSpec(memory_space=pl.ANY)
    return pl.pallas_call(
        functools.partial(join_kernel, chunk, len(sources)),
        in_specs=[whole] * (len(sources) + len(joined)),
        out_specs=whole,
        out_shape=jax.ShapeDtypeStruct((CHUNKS * TILE, width), jnp.bfloat16),
        input_output_aliases={len(sources): 0} if joined else {},
        scratch_shapes=[
            pltpu.VMEM((TILE, width), jnp.bfloat16),
            pltpu.SemaphoreType.DMA((heads,)),
            pltpu.SemaphoreType.DMA,
        ],
        compiler_params=pltpu.CompilerParams(vmem_limit_bytes=8 * MIB),
        cost_estimate=pl.CostEstimate(flops=0, bytes_accessed=4 * MIB, transcendentals=0),
    )(*sources, *joined)


def attend_kernel(
    chunk,
    slot_ids,
    query_hbm,
    left_hbm,
    own_hbm,
    right_hbm,
    *refs,
):
    out_refs, (keys, values, query, marks, scores, tops, sems) = refs[:-7], refs[-7:]
    pairs = own_hbm.shape[0]
    rim = left_hbm.shape[0]
    places = ((own_hbm, rim), (left_hbm, 0), (right_hbm, rim + pairs))
    copies = [pltpu.make_async_copy(query_hbm, query, sems.at[0])]
    for part, held in enumerate((keys, values)):
        for source, start in places:
            copies.append(
                pltpu.make_async_copy(
                    source.at[:, pl.ds(part * CHUNKS, CHUNKS)],
                    held.at[pl.ds(start, source.shape[0])],
                    sems.at[len(copies)],
                )
            )
    for copy in copies:
        copy.start()
    marks[0] = jnp.ones((TILE, HEAD_DIM), jnp.bfloat16)
    marks[1] = jnp.zeros((TILE, HEAD_DIM), jnp.bfloat16)
    values[NO_TILE // CHUNKS] = jnp.zeros((CHUNKS, TILE, HEAD_DIM), jnp.bfloat16)
    for copy in copies[:4]:
        copy.wait()
    here_x = lax.axis_index("seq") >> 3

    def pair_of(turn, by):
        return (((here_x + by) & 3) << 3) + turn

    def score_pair(row, tile_query, slot):
        ids = [slot_ids[0, slot + i, row] for i in range(2)]
        both = jnp.concatenate([keys[k >> 1, k & 1] for k in ids], axis=0)
        return lax.dot_general(
            tile_query, both, (((1,), (1,)), ((), ())), preferred_element_type=jnp.float32
        )

    def value_pair(row, slot):
        ids = [slot_ids[1, slot + i, row] for i in range(2)]
        return jnp.concatenate(
            [jnp.concatenate([values[k >> 1, k & 1], marks[k >> 7]], axis=1) for k in ids], axis=0
        )

    def fold(best, score):
        score = jnp.maximum(score[:, :TILE], score[:, TILE:])
        return score if best is None else jnp.maximum(best, score)

    def put_top(place, best):
        tops[place] = jnp.broadcast_to(jnp.max(best, axis=1, keepdims=True), (TILE, TILE))

    best = None
    first_row = pair_of(0, 0) * CHUNKS + chunk
    for slot in range(0, KSEL, 2):
        score = score_pair(first_row, query[0], slot)
        scores[0, slot // 2] = score
        best = fold(best, score)
    put_top(0, best)
    for copy in copies[4:]:
        copy.wait()

    def step(turn, carry):
        for by in range(ALONG_X):
            now = by % 2
            later_by = (by + 1) % ALONG_X
            later_turn = turn if later_by else jnp.minimum(turn + 1, ALONG_Z - 1)
            tile = turn * ALONG_X + -by % ALONG_X
            later = later_turn * ALONG_X + -later_by % ALONG_X
            row = pair_of(turn, by) * CHUNKS + chunk
            later_row = pair_of(later_turn, later_by) * CHUNKS + chunk
            top = tops[now]
            top = jnp.concatenate([top, top], axis=1)
            later_query = query[later]
            best = None
            mixed = None
            for slot in range(0, KSEL, 2):
                score = score_pair(later_row, later_query, slot)
                scores[1 - now, slot // 2] = score
                best = fold(best, score)
                weights = jnp.exp2((scores[now, slot // 2] - top) * EXP2_SCALE)
                part = jnp.dot(
                    weights.astype(jnp.bfloat16),
                    value_pair(row, slot),
                    preferred_element_type=jnp.float32,
                )
                mixed = part if mixed is None else mixed + part
            put_top(1 - now, best)
            tile_out = (mixed[:, :HEAD_DIM] / mixed[:, HEAD_DIM:]).astype(jnp.bfloat16)
            if len(out_refs) == 1:
                out_refs[0][tile] = tile_out
            else:
                out_refs[by][turn, 0] = tile_out
        return carry

    lax.fori_loop(0, ALONG_Z, step, 0)


def attend(chunk, outs, ids, query_tiles, left, own, right):
    count = query_tiles.shape[0]
    shape = (count, TILE, HEAD_DIM) if outs == 1 else (count // outs, 1, TILE, HEAD_DIM)
    held = own.shape[0] + 2 * left.shape[0]
    whole = pl.BlockSpec(memory_space=pl.ANY)
    scalar = pl.BlockSpec(memory_space=pltpu.SMEM)
    return pl.pallas_call(
        functools.partial(attend_kernel, chunk),
        in_specs=[scalar, whole, whole, whole, whole],
        out_specs=[pl.BlockSpec(memory_space=pltpu.VMEM)] * outs,
        out_shape=[jax.ShapeDtypeStruct(shape, jnp.bfloat16)] * outs,
        scratch_shapes=[
            pltpu.VMEM((held, CHUNKS, TILE, HEAD_DIM), jnp.bfloat16),
            pltpu.VMEM((held + 1, CHUNKS, TILE, HEAD_DIM), jnp.bfloat16),
            pltpu.VMEM((count, TILE, HEAD_DIM), jnp.bfloat16),
            pltpu.VMEM((2, TILE, HEAD_DIM), jnp.bfloat16),
            pltpu.VMEM((2, KSEL // 2, TILE, 2 * TILE), jnp.float32),
            pltpu.VMEM((2, TILE, TILE), jnp.float32),
            pltpu.SemaphoreType.DMA((7,)),
        ],
        compiler_params=pltpu.CompilerParams(vmem_limit_bytes=16 * MIB),
        cost_estimate=pl.CostEstimate(
            flops=count * KSEL * TILE * TILE * HEAD_DIM * 4,
            bytes_accessed=12 * MIB,
            transcendentals=count * KSEL * TILE * TILE,
        ),
    )(ids, query_tiles, left, own, right)


def exchange(blocks):
    return lax.all_to_all(blocks, "seq", split_axis=0, concat_axis=0, tiled=True)


def exchange_z(blocks):
    groups = [[x * ALONG_Z + z for z in range(ALONG_Z)] for x in range(ALONG_X)]
    return lax.all_to_all(
        blocks, "seq", split_axis=0, concat_axis=0, tiled=True, axis_index_groups=groups
    )


def shift_x(blocks, by):
    pairs = [
        (x * ALONG_Z + z, (x + by) % ALONG_X * ALONG_Z + z)
        for x in range(ALONG_X)
        for z in range(ALONG_Z)
    ]
    return lax.ppermute(blocks, "seq", pairs)


def queries_by_x(queries):
    blocks = split_queries(queries)
    x = lax.axis_index("seq") // ALONG_Z
    parts = []
    for by in range(ALONG_X):
        start = (x + by) % ALONG_X * ALONG_Z
        part = lax.dynamic_slice_in_dim(blocks, start, ALONG_Z, axis=0)
        parts.append(shift_x(part, by) if by else part)
    return [
        jnp.stack([part[:, chunk] for part in parts], axis=1).reshape(-1, TILE, HEAD_DIM)
        for chunk in range(CHUNKS)
    ]


def outputs_by_x(blocks):
    blocks = blocks.reshape(ALONG_Z, ALONG_X, TILE, HEAD_DIM)
    return [
        shift_x(blocks[:, by], ALONG_X - by) if by else blocks[:, by] for by in range(ALONG_X)
    ]


def per_device(queries, keys_values, extents, tile_lists):
    seq_size = lax.axis_size("seq")
    tm_size = lax.axis_size("tm")
    blocks, ids = split_pairs(keys_values, extents, tile_lists)
    first, second = queries_by_x(queries)
    own = exchange(blocks)
    half = seq_size // 2
    ends = tm_size - 1
    left = lax.ppermute(own[half:], "tm", [(i, i + 1) for i in range(ends)])
    right = lax.ppermute(own[:half], "tm", [(i + 1, i) for i in range(ends)])
    first = exchange_z(first)
    second = exchange_z(second)
    (first_out,) = attend(0, 1, ids, first, left, own, right)
    first_out = outputs_by_x(exchange_z(first_out))
    second_out = attend(1, ALONG_X, ids, second, left, own, right)
    second_out = [shift_x(part, by) if by else part for by, part in enumerate(second_out)]
    second_out = exchange_z(jnp.concatenate(second_out, axis=1).reshape(-1, TILE, HEAD_DIM))
    return join_heads(1, [second_out], join_heads(0, first_out))


def solution(mesh):
    placed = (P(("tm", "seq"), None), P(None, ("tm", "seq"), None), P(), P("tm", None))
    return jax.shard_map(
        per_device, mesh=mesh, in_specs=placed, out_specs=P(("tm", "seq"), None), check_vma=False
    )
```

```python
import functools

import jax
import jax.numpy as jnp
from jax import lax
from jax.experimental import pallas as pl
from jax.experimental.pallas import tpu as pltpu
from jax.sharding import PartitionSpec as P

HEAD_DIM = 128
TILE = 128
FRAME = 32
KSEL = 16
CHUNKS = 2
HEADS_STEP = 16
NO_TILE = 128
ALONG_X = 4
ALONG_Z = 8
EXP2_SCALE = HEAD_DIM ** (-0.5) * 1.4426950408889634
MIB = 1024 * 1024


def split_queries_kernel(query_ref, block_ref):
    for head in range(block_ref.shape[0]):
        columns = slice(head * HEAD_DIM, (head + 1) * HEAD_DIM)
        for chunk in range(CHUNKS):
            block_ref[head, chunk] = query_ref[chunk * TILE : (chunk + 1) * TILE, columns]


def split_queries(queries):
    tok_dev, width_all = queries.shape
    heads = width_all // HEAD_DIM
    return pl.pallas_call(
        split_queries_kernel,
        grid=(heads // HEADS_STEP,),
        in_specs=[pl.BlockSpec((tok_dev, HEADS_STEP * HEAD_DIM), lambda i: (0, i))],
        out_specs=pl.BlockSpec((HEADS_STEP, CHUNKS, TILE, HEAD_DIM), lambda i: (i, 0, 0, 0)),
        out_shape=jax.ShapeDtypeStruct((heads, CHUNKS, TILE, HEAD_DIM), jnp.bfloat16),
        compiler_params=pltpu.CompilerParams(vmem_limit_bytes=60 * MIB),
        cost_estimate=pl.CostEstimate(flops=0, bytes_accessed=4 * MIB, transcendentals=0),
    )(queries)


def split_pairs_kernel(extents, list_ref, pair_ref, block_ref, id_ref):
    for head in range(block_ref.shape[0]):
        columns = slice(head * HEAD_DIM, (head + 1) * HEAD_DIM)
        for part in range(2):
            for half in range(CHUNKS):
                rows = slice(half * TILE, (half + 1) * TILE)
                block_ref[head, part * CHUNKS + half] = pair_ref[part, rows, columns]

    @pl.when(pl.program_id(0) == 0)
    def _():
        head = lax.axis_index("seq")
        listed = list_ref[...]
        first = lax.axis_index("tm") * listed.shape[1]
        tiles = first + lax.broadcasted_iota(jnp.int32, listed.shape, 1)
        live = None
        for axis, (low, mask) in enumerate(((5, 15), (3, 3), (0, 7))):
            gap = jnp.abs(((listed >> low) & mask) - ((tiles >> low) & mask))
            near = gap <= extents[axis, head]
            live = near if live is None else live & near
        shift = first - FRAME
        id_ref[0] = jnp.where(live, listed, tiles) - shift
        id_ref[1] = jnp.where(live, listed - shift, NO_TILE)


def split_pairs(keys_values, extents, tile_lists):
    _, tok_dev, width_all = keys_values.shape
    heads = width_all // HEAD_DIM
    parts = 2 * CHUNKS
    rows, slots = tile_lists.shape
    return pl.pallas_call(
        split_pairs_kernel,
        grid=(heads // HEADS_STEP,),
        in_specs=[
            pl.BlockSpec(memory_space=pltpu.SMEM),
            pl.BlockSpec((slots, rows), lambda i: (0, 0)),
            pl.BlockSpec((2, tok_dev, HEADS_STEP * HEAD_DIM), lambda i: (0, 0, i)),
        ],
        out_specs=[
            pl.BlockSpec((HEADS_STEP, parts, TILE, HEAD_DIM), lambda i: (i, 0, 0, 0)),
            pl.BlockSpec((2, slots, rows), lambda i: (0, 0, 0)),
        ],
        out_shape=[
            jax.ShapeDtypeStruct((heads, parts, TILE, HEAD_DIM), jnp.bfloat16),
            jax.ShapeDtypeStruct((2, slots, rows), jnp.int32),
        ],
        compiler_params=pltpu.CompilerParams(vmem_limit_bytes=60 * MIB),
    )(extents, tile_lists.T, keys_values)


def join_kernel(chunk, count, *refs):
    sources, (out_hbm, held, in_sems, out_sem) = refs[:count], refs[-4:]
    here_x = lax.axis_index("seq") >> 3
    reads = []
    for by, source_hbm in enumerate(sources):
        for place in range(source_hbm.shape[0]):
            head = place if count == 1 else ((here_x + by) & 3) * ALONG_Z + place
            columns = pl.ds(pl.multiple_of(head * HEAD_DIM, HEAD_DIM), HEAD_DIM)
            reads.append(
                pltpu.make_async_copy(
                    source_hbm.at[place], held.at[:, columns], in_sems.at[len(reads)]
                )
            )
    for copy in reads:
        copy.start()
    for copy in reads:
        copy.wait()
    write = pltpu.make_async_copy(held, out_hbm.at[pl.ds(chunk * TILE, TILE)], out_sem)
    write.start()
    write.wait()


def join_heads(chunk, sources, *joined):
    heads = sum(source.shape[0] for source in sources)
    width = heads * HEAD_DIM
    whole = pl.BlockSpec(memory_space=pl.ANY)
    return pl.pallas_call(
        functools.partial(join_kernel, chunk, len(sources)),
        in_specs=[whole] * (len(sources) + len(joined)),
        out_specs=whole,
        out_shape=jax.ShapeDtypeStruct((CHUNKS * TILE, width), jnp.bfloat16),
        input_output_aliases={len(sources): 0} if joined else {},
        scratch_shapes=[
            pltpu.VMEM((TILE, width), jnp.bfloat16),
            pltpu.SemaphoreType.DMA((heads,)),
            pltpu.SemaphoreType.DMA,
        ],
        compiler_params=pltpu.CompilerParams(vmem_limit_bytes=8 * MIB),
        cost_estimate=pl.CostEstimate(flops=0, bytes_accessed=4 * MIB, transcendentals=0),
    )(*sources, *joined)


def attend_kernel(
    chunk,
    slot_ids,
    query_hbm,
    left_hbm,
    own_hbm,
    right_hbm,
    out_ref,
    keys,
    values,
    query,
    marks,
    scores,
    tops,
    sems,
):
    pairs = own_hbm.shape[0]
    rim = left_hbm.shape[0]
    places = ((own_hbm, rim), (left_hbm, 0), (right_hbm, rim + pairs))
    copies = [pltpu.make_async_copy(query_hbm, query, sems.at[0])]
    for part, held in enumerate((keys, values)):
        for source, start in places:
            copies.append(
                pltpu.make_async_copy(
                    source.at[:, pl.ds(part * CHUNKS, CHUNKS)],
                    held.at[pl.ds(start, source.shape[0])],
                    sems.at[len(copies)],
                )
            )
    for copy in copies:
        copy.start()
    marks[0] = jnp.ones((TILE, HEAD_DIM), jnp.bfloat16)
    marks[1] = jnp.zeros((TILE, HEAD_DIM), jnp.bfloat16)
    values[NO_TILE // CHUNKS] = jnp.zeros((CHUNKS, TILE, HEAD_DIM), jnp.bfloat16)
    for copy in copies[:4]:
        copy.wait()
    here_x = lax.axis_index("seq") >> 3

    def pair_of(turn, by):
        return (((here_x + by) & 3) << 3) + turn

    def score_pair(row, tile_query, slot):
        ids = [slot_ids[0, slot + i, row] for i in range(2)]
        both = jnp.concatenate([keys[k >> 1, k & 1] for k in ids], axis=0)
        return lax.dot_general(
            tile_query, both, (((1,), (1,)), ((), ())), preferred_element_type=jnp.float32
        )

    def value_pair(row, slot):
        ids = [slot_ids[1, slot + i, row] for i in range(2)]
        return jnp.concatenate(
            [jnp.concatenate([values[k >> 1, k & 1], marks[k >> 7]], axis=1) for k in ids], axis=0
        )

    def fold(best, score):
        score = jnp.maximum(score[:, :TILE], score[:, TILE:])
        return score if best is None else jnp.maximum(best, score)

    def put_top(place, best):
        tops[place] = jnp.broadcast_to(jnp.max(best, axis=1, keepdims=True), (TILE, TILE))

    best = None
    first_row = pair_of(0, 0) * CHUNKS + chunk
    for slot in range(0, KSEL, 2):
        score = score_pair(first_row, query[0], slot)
        scores[0, slot // 2] = score
        best = fold(best, score)
    put_top(0, best)
    for copy in copies[4:]:
        copy.wait()

    def step(turn, carry):
        for by in range(ALONG_X):
            now = by % 2
            later_by = (by + 1) % ALONG_X
            later_turn = turn if later_by else jnp.minimum(turn + 1, ALONG_Z - 1)
            tile = turn * ALONG_X + -by % ALONG_X
            later = later_turn * ALONG_X + -later_by % ALONG_X
            pair = pair_of(turn, by)
            row = pair * CHUNKS + chunk
            later_row = pair_of(later_turn, later_by) * CHUNKS + chunk
            top = tops[now]
            top = jnp.concatenate([top, top], axis=1)
            later_query = query[later]
            best = None
            mixed = None
            for slot in range(0, KSEL, 2):
                score = score_pair(later_row, later_query, slot)
                scores[1 - now, slot // 2] = score
                best = fold(best, score)
                weights = jnp.exp2((scores[now, slot // 2] - top) * EXP2_SCALE)
                part = jnp.dot(
                    weights.astype(jnp.bfloat16),
                    value_pair(row, slot),
                    preferred_element_type=jnp.float32,
                )
                mixed = part if mixed is None else mixed + part
            put_top(1 - now, best)
            out_ref[tile if chunk == 0 else pair] = (mixed[:, :HEAD_DIM] / mixed[:, HEAD_DIM:]).astype(jnp.bfloat16)
        return carry

    lax.fori_loop(0, ALONG_Z, step, 0)


def attend(chunk, ids, query_tiles, left, own, right):
    count = query_tiles.shape[0]
    held = own.shape[0] + 2 * left.shape[0]
    whole = pl.BlockSpec(memory_space=pl.ANY)
    scalar = pl.BlockSpec(memory_space=pltpu.SMEM)
    return pl.pallas_call(
        functools.partial(attend_kernel, chunk),
        in_specs=[scalar, whole, whole, whole, whole],
        out_specs=pl.BlockSpec(memory_space=pltpu.VMEM),
        out_shape=jax.ShapeDtypeStruct((count, TILE, HEAD_DIM), jnp.bfloat16),
        scratch_shapes=[
            pltpu.VMEM((held, CHUNKS, TILE, HEAD_DIM), jnp.bfloat16),
            pltpu.VMEM((held + 1, CHUNKS, TILE, HEAD_DIM), jnp.bfloat16),
            pltpu.VMEM((count, TILE, HEAD_DIM), jnp.bfloat16),
            pltpu.VMEM((2, TILE, HEAD_DIM), jnp.bfloat16),
            pltpu.VMEM((2, KSEL // 2, TILE, 2 * TILE), jnp.float32),
            pltpu.VMEM((2, TILE, TILE), jnp.float32),
            pltpu.SemaphoreType.DMA((7,)),
        ],
        compiler_params=pltpu.CompilerParams(vmem_limit_bytes=16 * MIB),
        cost_estimate=pl.CostEstimate(
            flops=count * KSEL * TILE * TILE * HEAD_DIM * 4,
            bytes_accessed=12 * MIB,
            transcendentals=count * KSEL * TILE * TILE,
        ),
    )(ids, query_tiles, left, own, right)


def exchange(blocks):
    return lax.all_to_all(blocks, "seq", split_axis=0, concat_axis=0, tiled=True)


def exchange_z(blocks):
    groups = [[x * ALONG_Z + z for z in range(ALONG_Z)] for x in range(ALONG_X)]
    return lax.all_to_all(
        blocks, "seq", split_axis=0, concat_axis=0, tiled=True, axis_index_groups=groups
    )


def shift_x(blocks, by):
    pairs = [
        (x * ALONG_Z + z, (x + by) % ALONG_X * ALONG_Z + z)
        for x in range(ALONG_X)
        for z in range(ALONG_Z)
    ]
    return lax.ppermute(blocks, "seq", pairs)


def queries_by_x(queries):
    blocks = split_queries(queries)
    x = lax.axis_index("seq") // ALONG_Z
    parts = []
    for by in range(ALONG_X):
        start = (x + by) % ALONG_X * ALONG_Z
        part = lax.dynamic_slice_in_dim(blocks, start, ALONG_Z, axis=0)
        parts.append(shift_x(part, by) if by else part)
    return [
        jnp.stack([part[:, chunk] for part in parts], axis=1).reshape(-1, TILE, HEAD_DIM)
        for chunk in range(CHUNKS)
    ]


def outputs_by_x(blocks):
    blocks = blocks.reshape(ALONG_Z, ALONG_X, TILE, HEAD_DIM)
    return [
        shift_x(blocks[:, by], ALONG_X - by) if by else blocks[:, by] for by in range(ALONG_X)
    ]


def per_device(queries, keys_values, extents, tile_lists):
    seq_size = lax.axis_size("seq")
    tm_size = lax.axis_size("tm")
    blocks, ids = split_pairs(keys_values, extents, tile_lists)
    first, second = queries_by_x(queries)
    own = exchange(blocks)
    half = seq_size // 2
    ends = tm_size - 1
    left = lax.ppermute(own[half:], "tm", [(i, i + 1) for i in range(ends)])
    right = lax.ppermute(own[:half], "tm", [(i + 1, i) for i in range(ends)])
    first = exchange_z(first)
    second = exchange_z(second)
    first_out = exchange_z(attend(0, ids, first, left, own, right))
    first_out = outputs_by_x(first_out)
    second_out = exchange(attend(1, ids, second, left, own, right))
    return join_heads(1, [second_out], join_heads(0, first_out))


def solution(mesh):
    placed = (P(("tm", "seq"), None), P(None, ("tm", "seq"), None), P(), P("tm", None))
    return jax.shard_map(
        per_device, mesh=mesh, in_specs=placed, out_specs=P(("tm", "seq"), None), check_vma=False
    )
```

```python
import functools

import jax
import jax.numpy as jnp
from jax import lax
from jax.experimental import pallas as pl
from jax.experimental.pallas import tpu as pltpu
from jax.sharding import PartitionSpec as P

HEAD_DIM = 128
TILE = 128
FRAME = 32
KSEL = 16
CHUNKS = 2
HEADS_STEP = 16
NO_TILE = 128
ALONG_X = 4
ALONG_Z = 8
EXP2_SCALE = HEAD_DIM ** (-0.5) * 1.4426950408889634
MIB = 1024 * 1024


def split_queries_kernel(query_ref, block_ref):
    for head in range(block_ref.shape[0]):
        columns = slice(head * HEAD_DIM, (head + 1) * HEAD_DIM)
        for chunk in range(CHUNKS):
            block_ref[head, chunk] = query_ref[chunk * TILE : (chunk + 1) * TILE, columns]


def split_queries(queries):
    tok_dev, width_all = queries.shape
    heads = width_all // HEAD_DIM
    return pl.pallas_call(
        split_queries_kernel,
        grid=(heads // HEADS_STEP,),
        in_specs=[pl.BlockSpec((tok_dev, HEADS_STEP * HEAD_DIM), lambda i: (0, i))],
        out_specs=pl.BlockSpec((HEADS_STEP, CHUNKS, TILE, HEAD_DIM), lambda i: (i, 0, 0, 0)),
        out_shape=jax.ShapeDtypeStruct((heads, CHUNKS, TILE, HEAD_DIM), jnp.bfloat16),
        compiler_params=pltpu.CompilerParams(vmem_limit_bytes=60 * MIB),
        cost_estimate=pl.CostEstimate(flops=0, bytes_accessed=4 * MIB, transcendentals=0),
    )(queries)


def split_pairs_kernel(extents, list_ref, pair_ref, block_ref, id_ref):
    for head in range(block_ref.shape[0]):
        columns = slice(head * HEAD_DIM, (head + 1) * HEAD_DIM)
        for part in range(2):
            for half in range(CHUNKS):
                rows = slice(half * TILE, (half + 1) * TILE)
                block_ref[head, part * CHUNKS + half] = pair_ref[part, rows, columns]

    @pl.when(pl.program_id(0) == 0)
    def _():
        head = lax.axis_index("seq")
        listed = list_ref[...]
        first = lax.axis_index("tm") * listed.shape[1]
        tiles = first + lax.broadcasted_iota(jnp.int32, listed.shape, 1)
        live = None
        for axis, (low, mask) in enumerate(((5, 15), (3, 3), (0, 7))):
            gap = jnp.abs(((listed >> low) & mask) - ((tiles >> low) & mask))
            near = gap <= extents[axis, head]
            live = near if live is None else live & near
        shift = first - FRAME
        id_ref[0] = jnp.where(live, listed, tiles) - shift
        id_ref[1] = jnp.where(live, listed - shift, NO_TILE)


def split_pairs(keys_values, extents, tile_lists):
    _, tok_dev, width_all = keys_values.shape
    heads = width_all // HEAD_DIM
    parts = 2 * CHUNKS
    rows, slots = tile_lists.shape
    return pl.pallas_call(
        split_pairs_kernel,
        grid=(heads // HEADS_STEP,),
        in_specs=[
            pl.BlockSpec(memory_space=pltpu.SMEM),
            pl.BlockSpec((slots, rows), lambda i: (0, 0)),
            pl.BlockSpec((2, tok_dev, HEADS_STEP * HEAD_DIM), lambda i: (0, 0, i)),
        ],
        out_specs=[
            pl.BlockSpec((HEADS_STEP, parts, TILE, HEAD_DIM), lambda i: (i, 0, 0, 0)),
            pl.BlockSpec((2, slots, rows), lambda i: (0, 0, 0)),
        ],
        out_shape=[
            jax.ShapeDtypeStruct((heads, parts, TILE, HEAD_DIM), jnp.bfloat16),
            jax.ShapeDtypeStruct((2, slots, rows), jnp.int32),
        ],
        compiler_params=pltpu.CompilerParams(vmem_limit_bytes=60 * MIB),
    )(extents, tile_lists.T, keys_values)


def join_kernel(chunk, count, *refs):
    sources, (out_hbm, held, in_sems, out_sem) = refs[:count], refs[-4:]
    here_x = lax.axis_index("seq") >> 3
    reads = []
    for by, source_hbm in enumerate(sources):
        for place in range(source_hbm.shape[0]):
            head = place if count == 1 else ((here_x + by) & 3) * ALONG_Z + place
            columns = pl.ds(pl.multiple_of(head * HEAD_DIM, HEAD_DIM), HEAD_DIM)
            reads.append(
                pltpu.make_async_copy(
                    source_hbm.at[place], held.at[:, columns], in_sems.at[len(reads)]
                )
            )
    for copy in reads:
        copy.start()
    for copy in reads:
        copy.wait()
    write = pltpu.make_async_copy(held, out_hbm.at[pl.ds(chunk * TILE, TILE)], out_sem)
    write.start()
    write.wait()


def join_heads(chunk, sources, *joined):
    heads = sum(source.shape[0] for source in sources)
    width = heads * HEAD_DIM
    whole = pl.BlockSpec(memory_space=pl.ANY)
    return pl.pallas_call(
        functools.partial(join_kernel, chunk, len(sources)),
        in_specs=[whole] * (len(sources) + len(joined)),
        out_specs=whole,
        out_shape=jax.ShapeDtypeStruct((CHUNKS * TILE, width), jnp.bfloat16),
        input_output_aliases={len(sources): 0} if joined else {},
        scratch_shapes=[
            pltpu.VMEM((TILE, width), jnp.bfloat16),
            pltpu.SemaphoreType.DMA((heads,)),
            pltpu.SemaphoreType.DMA,
        ],
        compiler_params=pltpu.CompilerParams(vmem_limit_bytes=8 * MIB),
        cost_estimate=pl.CostEstimate(flops=0, bytes_accessed=4 * MIB, transcendentals=0),
    )(*sources, *joined)


def attend_kernel(
    chunk,
    slot_ids,
    query_hbm,
    left_hbm,
    own_hbm,
    right_hbm,
    out_ref,
    keys,
    values,
    query,
    marks,
    scores,
    tops,
    sems,
):
    pairs = own_hbm.shape[0]
    rim = left_hbm.shape[0]
    places = ((own_hbm, rim), (left_hbm, 0), (right_hbm, rim + pairs))
    copies = [pltpu.make_async_copy(query_hbm, query, sems.at[0])]
    for part, held in enumerate((keys, values)):
        for source, start in places:
            copies.append(
                pltpu.make_async_copy(
                    source.at[:, pl.ds(part * CHUNKS, CHUNKS)],
                    held.at[pl.ds(start, source.shape[0])],
                    sems.at[len(copies)],
                )
            )
    for copy in copies:
        copy.start()
    marks[0] = jnp.ones((TILE, HEAD_DIM), jnp.bfloat16)
    marks[1] = jnp.zeros((TILE, HEAD_DIM), jnp.bfloat16)
    values[NO_TILE // CHUNKS] = jnp.zeros((CHUNKS, TILE, HEAD_DIM), jnp.bfloat16)
    for copy in copies[:4]:
        copy.wait()
    here_x = lax.axis_index("seq") >> 3

    def pair_of(turn, by):
        return (((here_x + by) & 3) << 3) + turn

    here_z = lax.axis_index("seq") & 7

    def query_of(turn, by):
        place = (here_z - turn) & 7 if chunk == 0 else turn
        return place * ALONG_X + -by % ALONG_X

    def score_pair(row, tile_query, slot):
        ids = [slot_ids[0, slot + i, row] for i in range(2)]
        both = jnp.concatenate([keys[k >> 1, k & 1] for k in ids], axis=0)
        return lax.dot_general(
            tile_query, both, (((1,), (1,)), ((), ())), preferred_element_type=jnp.float32
        )

    def value_pair(row, slot):
        ids = [slot_ids[1, slot + i, row] for i in range(2)]
        return jnp.concatenate(
            [jnp.concatenate([values[k >> 1, k & 1], marks[k >> 7]], axis=1) for k in ids], axis=0
        )

    def fold(best, score):
        score = jnp.maximum(score[:, :TILE], score[:, TILE:])
        return score if best is None else jnp.maximum(best, score)

    def put_top(place, best):
        tops[place] = jnp.broadcast_to(jnp.max(best, axis=1, keepdims=True), (TILE, TILE))

    best = None
    first_row = pair_of(0, 0) * CHUNKS + chunk
    for slot in range(0, KSEL, 2):
        score = score_pair(first_row, query[query_of(0, 0)], slot)
        scores[0, slot // 2] = score
        best = fold(best, score)
    put_top(0, best)
    for copy in copies[4:]:
        copy.wait()

    def step(turn, carry):
        for by in range(ALONG_X):
            now = by % 2
            later_by = (by + 1) % ALONG_X
            later_turn = turn if later_by else jnp.minimum(turn + 1, ALONG_Z - 1)
            tile = turn * ALONG_X + -by % ALONG_X
            later = query_of(later_turn, later_by)
            pair = pair_of(turn, by)
            row = pair * CHUNKS + chunk
            later_row = pair_of(later_turn, later_by) * CHUNKS + chunk
            top = tops[now]
            top = jnp.concatenate([top, top], axis=1)
            later_query = query[later]
            best = None
            mixed = None
            for slot in range(0, KSEL, 2):
                score = score_pair(later_row, later_query, slot)
                scores[1 - now, slot // 2] = score
                best = fold(best, score)
                weights = jnp.exp2((scores[now, slot // 2] - top) * EXP2_SCALE)
                part = jnp.dot(
                    weights.astype(jnp.bfloat16),
                    value_pair(row, slot),
                    preferred_element_type=jnp.float32,
                )
                mixed = part if mixed is None else mixed + part
            put_top(1 - now, best)
            out_ref[tile if chunk == 0 else pair] = (mixed[:, :HEAD_DIM] / mixed[:, HEAD_DIM:]).astype(jnp.bfloat16)
        return carry

    lax.fori_loop(0, ALONG_Z, step, 0)


def attend(chunk, ids, query_tiles, left, own, right):
    count = query_tiles.shape[0]
    held = own.shape[0] + 2 * left.shape[0]
    whole = pl.BlockSpec(memory_space=pl.ANY)
    scalar = pl.BlockSpec(memory_space=pltpu.SMEM)
    return pl.pallas_call(
        functools.partial(attend_kernel, chunk),
        in_specs=[scalar, whole, whole, whole, whole],
        out_specs=pl.BlockSpec(memory_space=pltpu.VMEM),
        out_shape=jax.ShapeDtypeStruct((count, TILE, HEAD_DIM), jnp.bfloat16),
        scratch_shapes=[
            pltpu.VMEM((held, CHUNKS, TILE, HEAD_DIM), jnp.bfloat16),
            pltpu.VMEM((held + 1, CHUNKS, TILE, HEAD_DIM), jnp.bfloat16),
            pltpu.VMEM((count, TILE, HEAD_DIM), jnp.bfloat16),
            pltpu.VMEM((2, TILE, HEAD_DIM), jnp.bfloat16),
            pltpu.VMEM((2, KSEL // 2, TILE, 2 * TILE), jnp.float32),
            pltpu.VMEM((2, TILE, TILE), jnp.float32),
            pltpu.SemaphoreType.DMA((7,)),
        ],
        compiler_params=pltpu.CompilerParams(vmem_limit_bytes=16 * MIB),
        cost_estimate=pl.CostEstimate(
            flops=count * KSEL * TILE * TILE * HEAD_DIM * 4,
            bytes_accessed=12 * MIB,
            transcendentals=count * KSEL * TILE * TILE,
        ),
    )(ids, query_tiles, left, own, right)


def exchange(blocks):
    return lax.all_to_all(blocks, "seq", split_axis=0, concat_axis=0, tiled=True)


def exchange_z(blocks):
    groups = [[x * ALONG_Z + z for z in range(ALONG_Z)] for x in range(ALONG_X)]
    return lax.all_to_all(
        blocks, "seq", split_axis=0, concat_axis=0, tiled=True, axis_index_groups=groups
    )


def shift_x(blocks, by):
    pairs = [
        (x * ALONG_Z + z, (x + by) % ALONG_X * ALONG_Z + z)
        for x in range(ALONG_X)
        for z in range(ALONG_Z)
    ]
    return lax.ppermute(blocks, "seq", pairs)


def queries_by_x(queries):
    blocks = split_queries(queries)
    x = lax.axis_index("seq") // ALONG_Z
    parts = []
    for by in range(ALONG_X):
        start = (x + by) % ALONG_X * ALONG_Z
        part = lax.dynamic_slice_in_dim(blocks, start, ALONG_Z, axis=0)
        parts.append(shift_x(part, by) if by else part)
    return [
        jnp.stack([part[:, chunk] for part in parts], axis=1).reshape(-1, TILE, HEAD_DIM)
        for chunk in range(CHUNKS)
    ]


def shift_z(blocks, by):
    pairs = [
        (x * ALONG_Z + z, x * ALONG_Z + (z + by) % ALONG_Z)
        for x in range(ALONG_X)
        for z in range(ALONG_Z)
    ]
    return lax.ppermute(blocks, "seq", pairs)


def queries_by_z(blocks):
    blocks = blocks.reshape(ALONG_Z, ALONG_X, TILE, HEAD_DIM)
    z = lax.axis_index("seq") % ALONG_Z
    parts = [None] * ALONG_Z
    for by in (0, 4, 3, 5, 2, 6, 1, 7):
        part = lax.dynamic_slice_in_dim(blocks, (z + by) % ALONG_Z, 1, axis=0)
        parts[by] = shift_z(part, by) if by else part
    return jnp.concatenate(parts, axis=0).reshape(-1, TILE, HEAD_DIM)


def outputs_by_x(blocks):
    blocks = blocks.reshape(ALONG_Z, ALONG_X, TILE, HEAD_DIM)
    return [
        shift_x(blocks[:, by], ALONG_X - by) if by else blocks[:, by] for by in range(ALONG_X)
    ]


def per_device(queries, keys_values, extents, tile_lists):
    seq_size = lax.axis_size("seq")
    tm_size = lax.axis_size("tm")
    blocks, ids = split_pairs(keys_values, extents, tile_lists)
    first, second = queries_by_x(queries)
    own = exchange(blocks)
    first = queries_by_z(first)
    own, first = lax.optimization_barrier((own, first))
    half = seq_size // 2
    ends = tm_size - 1
    left = lax.ppermute(own[half:], "tm", [(i, i + 1) for i in range(ends)])
    right = lax.ppermute(own[:half], "tm", [(i + 1, i) for i in range(ends)])
    second = exchange_z(second)
    first_out = exchange_z(attend(0, ids, first, left, own, right))
    first_out = outputs_by_x(first_out)
    second_out = exchange(attend(1, ids, second, left, own, right))
    return join_heads(1, [second_out], join_heads(0, first_out))


def solution(mesh):
    placed = (P(("tm", "seq"), None), P(None, ("tm", "seq"), None), P(), P("tm", None))
    return jax.shard_map(
        per_device, mesh=mesh, in_specs=placed, out_specs=P(("tm", "seq"), None), check_vma=False
    )
```

```python
import functools

import jax
import jax.numpy as jnp
from jax import lax
from jax.experimental import pallas as pl
from jax.experimental.pallas import tpu as pltpu
from jax.sharding import PartitionSpec as P

HEAD_DIM = 128
TILE = 128
FRAME = 32
KSEL = 16
CHUNKS = 2
HEADS_STEP = 16
NO_TILE = 128
ALONG_X = 4
ALONG_Z = 8
EXP2_SCALE = HEAD_DIM ** (-0.5) * 1.4426950408889634
MIB = 1024 * 1024


def split_queries_kernel(query_ref, block_ref):
    for head in range(block_ref.shape[0]):
        columns = slice(head * HEAD_DIM, (head + 1) * HEAD_DIM)
        for chunk in range(CHUNKS):
            block_ref[head, chunk] = query_ref[chunk * TILE : (chunk + 1) * TILE, columns]


def split_queries(queries):
    tok_dev, width_all = queries.shape
    heads = width_all // HEAD_DIM
    return pl.pallas_call(
        split_queries_kernel,
        grid=(heads // HEADS_STEP,),
        in_specs=[pl.BlockSpec((tok_dev, HEADS_STEP * HEAD_DIM), lambda i: (0, i))],
        out_specs=pl.BlockSpec((HEADS_STEP, CHUNKS, TILE, HEAD_DIM), lambda i: (i, 0, 0, 0)),
        out_shape=jax.ShapeDtypeStruct((heads, CHUNKS, TILE, HEAD_DIM), jnp.bfloat16),
        compiler_params=pltpu.CompilerParams(vmem_limit_bytes=60 * MIB),
        cost_estimate=pl.CostEstimate(flops=0, bytes_accessed=4 * MIB, transcendentals=0),
    )(queries)


def split_pairs_kernel(extents, list_ref, pair_ref, block_ref, id_ref):
    for head in range(block_ref.shape[0]):
        columns = slice(head * HEAD_DIM, (head + 1) * HEAD_DIM)
        for part in range(2):
            for half in range(CHUNKS):
                rows = slice(half * TILE, (half + 1) * TILE)
                block_ref[head, part * CHUNKS + half] = pair_ref[part, rows, columns]

    @pl.when(pl.program_id(0) == 0)
    def _():
        head = lax.axis_index("seq")
        listed = list_ref[...]
        first = lax.axis_index("tm") * listed.shape[1]
        tiles = first + lax.broadcasted_iota(jnp.int32, listed.shape, 1)
        live = None
        for axis, (low, mask) in enumerate(((5, 15), (3, 3), (0, 7))):
            gap = jnp.abs(((listed >> low) & mask) - ((tiles >> low) & mask))
            near = gap <= extents[axis, head]
            live = near if live is None else live & near
        shift = first - FRAME
        id_ref[0] = jnp.where(live, listed, tiles) - shift
        id_ref[1] = jnp.where(live, listed - shift, NO_TILE)


def split_pairs(keys_values, extents, tile_lists):
    _, tok_dev, width_all = keys_values.shape
    heads = width_all // HEAD_DIM
    parts = 2 * CHUNKS
    rows, slots = tile_lists.shape
    return pl.pallas_call(
        split_pairs_kernel,
        grid=(heads // HEADS_STEP,),
        in_specs=[
            pl.BlockSpec(memory_space=pltpu.SMEM),
            pl.BlockSpec((slots, rows), lambda i: (0, 0)),
            pl.BlockSpec((2, tok_dev, HEADS_STEP * HEAD_DIM), lambda i: (0, 0, i)),
        ],
        out_specs=[
            pl.BlockSpec((HEADS_STEP, parts, TILE, HEAD_DIM), lambda i: (i, 0, 0, 0)),
            pl.BlockSpec((2, slots, rows), lambda i: (0, 0, 0)),
        ],
        out_shape=[
            jax.ShapeDtypeStruct((heads, parts, TILE, HEAD_DIM), jnp.bfloat16),
            jax.ShapeDtypeStruct((2, slots, rows), jnp.int32),
        ],
        compiler_params=pltpu.CompilerParams(vmem_limit_bytes=60 * MIB),
    )(extents, tile_lists.T, keys_values)


def join_kernel(chunk, count, *refs):
    sources, (out_hbm, held, in_sems, out_sem) = refs[:count], refs[-4:]
    if count == 1:
        rows = pl.ds(chunk * TILE, TILE)
        writes = [
            pltpu.make_async_copy(
                sources[0].at[head],
                out_hbm.at[rows, pl.ds(head * HEAD_DIM, HEAD_DIM)],
                in_sems.at[head],
            )
            for head in range(sources[0].shape[0])
        ]
        for copy in writes:
            copy.start()
        for copy in writes:
            copy.wait()
        return
    here_x = lax.axis_index("seq") >> 3
    reads = []
    for by, source_hbm in enumerate(sources):
        for place in range(source_hbm.shape[0]):
            head = ((here_x + by) & 3) * ALONG_Z + place
            columns = pl.ds(pl.multiple_of(head * HEAD_DIM, HEAD_DIM), HEAD_DIM)
            reads.append(
                pltpu.make_async_copy(
                    source_hbm.at[place], held.at[:, columns], in_sems.at[len(reads)]
                )
            )
    for copy in reads:
        copy.start()
    for copy in reads:
        copy.wait()
    write = pltpu.make_async_copy(held, out_hbm.at[pl.ds(chunk * TILE, TILE)], out_sem)
    write.start()
    write.wait()


def join_heads(chunk, sources, *joined):
    heads = sum(source.shape[0] for source in sources)
    width = heads * HEAD_DIM
    whole = pl.BlockSpec(memory_space=pl.ANY)
    local = pl.BlockSpec(memory_space=pltpu.VMEM)
    return pl.pallas_call(
        functools.partial(join_kernel, chunk, len(sources)),
        in_specs=[local if joined else whole] * len(sources) + [whole] * len(joined),
        out_specs=whole,
        out_shape=jax.ShapeDtypeStruct((CHUNKS * TILE, width), jnp.bfloat16),
        input_output_aliases={len(sources): 0} if joined else {},
        scratch_shapes=[
            pltpu.VMEM((TILE, width), jnp.bfloat16),
            pltpu.SemaphoreType.DMA((heads,)),
            pltpu.SemaphoreType.DMA,
        ],
        compiler_params=pltpu.CompilerParams(vmem_limit_bytes=8 * MIB),
        cost_estimate=pl.CostEstimate(flops=0, bytes_accessed=4 * MIB, transcendentals=0),
    )(*sources, *joined)


def attend_kernel(
    chunk,
    slot_ids,
    query_hbm,
    left_hbm,
    own_hbm,
    right_hbm,
    out_ref,
    keys,
    values,
    query,
    marks,
    scores,
    tops,
    sems,
):
    pairs = own_hbm.shape[0]
    rim = left_hbm.shape[0]
    places = ((own_hbm, rim), (left_hbm, 0), (right_hbm, rim + pairs))
    copies = [pltpu.make_async_copy(query_hbm, query, sems.at[0])]
    for part, held in enumerate((keys, values)):
        for source, start in places:
            copies.append(
                pltpu.make_async_copy(
                    source.at[:, pl.ds(part * CHUNKS, CHUNKS)],
                    held.at[pl.ds(start, source.shape[0])],
                    sems.at[len(copies)],
                )
            )
    for copy in copies:
        copy.start()
    marks[0] = jnp.ones((TILE, HEAD_DIM), jnp.bfloat16)
    marks[1] = jnp.zeros((TILE, HEAD_DIM), jnp.bfloat16)
    values[NO_TILE // CHUNKS] = jnp.zeros((CHUNKS, TILE, HEAD_DIM), jnp.bfloat16)
    for copy in copies[:4]:
        copy.wait()
    here_x = lax.axis_index("seq") >> 3

    def pair_of(turn, by):
        return (((here_x + by) & 3) << 3) + turn

    def score_pair(row, tile_query, slot):
        ids = [slot_ids[0, slot + i, row] for i in range(2)]
        both = jnp.concatenate([keys[k >> 1, k & 1] for k in ids], axis=0)
        return lax.dot_general(
            tile_query, both, (((1,), (1,)), ((), ())), preferred_element_type=jnp.float32
        )

    def value_pair(row, slot):
        ids = [slot_ids[1, slot + i, row] for i in range(2)]
        return jnp.concatenate(
            [jnp.concatenate([values[k >> 1, k & 1], marks[k >> 7]], axis=1) for k in ids], axis=0
        )

    def fold(best, score):
        score = jnp.maximum(score[:, :TILE], score[:, TILE:])
        return score if best is None else jnp.maximum(best, score)

    def put_top(place, best):
        tops[place] = jnp.broadcast_to(jnp.max(best, axis=1, keepdims=True), (TILE, TILE))

    best = None
    first_row = pair_of(0, 0) * CHUNKS + chunk
    for slot in range(0, KSEL, 2):
        score = score_pair(first_row, query[0], slot)
        scores[0, slot // 2] = score
        best = fold(best, score)
    put_top(0, best)
    for copy in copies[4:]:
        copy.wait()

    def step(turn, carry):
        for by in range(ALONG_X):
            now = by % 2
            later_by = (by + 1) % ALONG_X
            later_turn = turn if later_by else jnp.minimum(turn + 1, ALONG_Z - 1)
            tile = turn * ALONG_X + -by % ALONG_X
            later = later_turn * ALONG_X + -later_by % ALONG_X
            pair = pair_of(turn, by)
            row = pair * CHUNKS + chunk
            later_row = pair_of(later_turn, later_by) * CHUNKS + chunk
            top = tops[now]
            top = jnp.concatenate([top, top], axis=1)
            later_query = query[later]
            best = None
            mixed = None
            for slot in range(0, KSEL, 2):
                score = score_pair(later_row, later_query, slot)
                scores[1 - now, slot // 2] = score
                best = fold(best, score)
                weights = jnp.exp2((scores[now, slot // 2] - top) * EXP2_SCALE)
                part = jnp.dot(
                    weights.astype(jnp.bfloat16),
                    value_pair(row, slot),
                    preferred_element_type=jnp.float32,
                )
                mixed = part if mixed is None else mixed + part
            put_top(1 - now, best)
            out_ref[tile if chunk == 0 else pair] = (mixed[:, :HEAD_DIM] / mixed[:, HEAD_DIM:]).astype(jnp.bfloat16)
        return carry

    lax.fori_loop(0, ALONG_Z, step, 0)


def attend(chunk, ids, query_tiles, left, own, right):
    count = query_tiles.shape[0]
    held = own.shape[0] + 2 * left.shape[0]
    whole = pl.BlockSpec(memory_space=pl.ANY)
    scalar = pl.BlockSpec(memory_space=pltpu.SMEM)
    return pl.pallas_call(
        functools.partial(attend_kernel, chunk),
        in_specs=[scalar, whole, whole, whole, whole],
        out_specs=pl.BlockSpec(memory_space=pltpu.VMEM),
        out_shape=jax.ShapeDtypeStruct((count, TILE, HEAD_DIM), jnp.bfloat16),
        scratch_shapes=[
            pltpu.VMEM((held, CHUNKS, TILE, HEAD_DIM), jnp.bfloat16),
            pltpu.VMEM((held + 1, CHUNKS, TILE, HEAD_DIM), jnp.bfloat16),
            pltpu.VMEM((count, TILE, HEAD_DIM), jnp.bfloat16),
            pltpu.VMEM((2, TILE, HEAD_DIM), jnp.bfloat16),
            pltpu.VMEM((2, KSEL // 2, TILE, 2 * TILE), jnp.float32),
            pltpu.VMEM((2, TILE, TILE), jnp.float32),
            pltpu.SemaphoreType.DMA((7,)),
        ],
        compiler_params=pltpu.CompilerParams(vmem_limit_bytes=16 * MIB),
        cost_estimate=pl.CostEstimate(
            flops=count * KSEL * TILE * TILE * HEAD_DIM * 4,
            bytes_accessed=12 * MIB,
            transcendentals=count * KSEL * TILE * TILE,
        ),
    )(ids, query_tiles, left, own, right)


def exchange(blocks):
    return lax.all_to_all(blocks, "seq", split_axis=0, concat_axis=0, tiled=True)


def exchange_z(blocks):
    groups = [[x * ALONG_Z + z for z in range(ALONG_Z)] for x in range(ALONG_X)]
    return lax.all_to_all(
        blocks, "seq", split_axis=0, concat_axis=0, tiled=True, axis_index_groups=groups
    )


def shift_x(blocks, by):
    pairs = [
        (x * ALONG_Z + z, (x + by) % ALONG_X * ALONG_Z + z)
        for x in range(ALONG_X)
        for z in range(ALONG_Z)
    ]
    return lax.ppermute(blocks, "seq", pairs)


def queries_by_x(queries):
    blocks = split_queries(queries)
    x = lax.axis_index("seq") // ALONG_Z
    parts = []
    for by in range(ALONG_X):
        start = (x + by) % ALONG_X * ALONG_Z
        part = lax.dynamic_slice_in_dim(blocks, start, ALONG_Z, axis=0)
        parts.append(shift_x(part, by) if by else part)
    return [
        jnp.stack([part[:, chunk] for part in parts], axis=1).reshape(-1, TILE, HEAD_DIM)
        for chunk in range(CHUNKS)
    ]


def outputs_by_x(blocks):
    blocks = blocks.reshape(ALONG_Z, ALONG_X, TILE, HEAD_DIM)
    return [
        shift_x(blocks[:, by], ALONG_X - by) if by else blocks[:, by] for by in range(ALONG_X)
    ]


def per_device(queries, keys_values, extents, tile_lists):
    seq_size = lax.axis_size("seq")
    tm_size = lax.axis_size("tm")
    blocks, ids = split_pairs(keys_values, extents, tile_lists)
    first, second = queries_by_x(queries)
    own = exchange(blocks)
    half = seq_size // 2
    ends = tm_size - 1
    left = lax.ppermute(own[half:], "tm", [(i, i + 1) for i in range(ends)])
    right = lax.ppermute(own[:half], "tm", [(i + 1, i) for i in range(ends)])
    first = exchange_z(first)
    second = exchange_z(second)
    first_out = exchange_z(attend(0, ids, first, left, own, right))
    first_out = outputs_by_x(first_out)
    second_out = exchange(attend(1, ids, second, left, own, right))
    return join_heads(1, [second_out], join_heads(0, first_out))


def solution(mesh):
    placed = (P(("tm", "seq"), None), P(None, ("tm", "seq"), None), P(), P("tm", None))
    return jax.shard_map(
        per_device, mesh=mesh, in_specs=placed, out_specs=P(("tm", "seq"), None), check_vma=False
    )
```
